512 devices in a mesh: ctx: 128 (over z_lo, x, y, core), tp: 4 (over z_hi).
Axes of the slice: x: 4, y: 8, z: 8 (z_hi: 4, z_lo: 2; z = z_hi * 2 + z_lo), core: 2. Of those that a mesh axis runs over, the one named last changes fastest.
Arguments:
- hidden_in: bfloat16 [4096, 2048], P('ctx'), may hold values from -6 to 6
- hidden_tan: bfloat16 [4096, 2048], P('ctx'), may hold values from -6 to 6
- qkv_weight: bfloat16 [3, 2048, 1024], P(None, None, 'tp'), may hold values from -0.125 to 0.125
- out_weight: bfloat16 [1024, 2048], P('tp'), may hold values from -0.1875 to 0.1875
- norm_gain: float32 [2, 128], replicated, may hold values from 0.5 to 6, as said below
- pos_local: int32 [2, 4096], P(None, 'ctx'), may hold values from 0 to 127
- tile_anchor: int32 [2, 128], P(None, 'ctx'), may hold values from 0 to 511
Outputs:
- attention_out: bfloat16 [4096, 2048], P('ctx', 'tp')
- attention_tan: bfloat16 [4096, 2048], P('ctx', 'tp')
The draws below stay inside these ranges and needn't reach their ends.
Inputs may be any that keep to these rules, and one draw needn't show every extreme that they name: `norm_gain`: positive gains.
All inputs are finite; a program needn't handle non-finite values.
Results may differ from the reference program's by a relative error of at most 0.035.
The reference program's roundings to bfloat16 on the way count: a program that leaves them out, or rounds other values in their place, can miss the bound.
Values may be sent and summed in bfloat16 or wider, within the bound.
A program may use at most 128 MiB of HBM per device.

```python
import jax
import jax.numpy as jnp
from jax import lax

D = 2048
HD = 128
TILE = 128
TOK_DEV = 32
SEQ = 4096
HW = 1024
N_CTX = 128


def draw_norm_gain(key, part):
    key = jax.random.fold_in(key, 7)
    return jnp.exp(jax.random.uniform(key, (2, HD), jnp.float32, jnp.log(0.6), jnp.log(1.6)))


def place_ends(drawn, rng, smallest, top_value):
    longest = drawn.shape.index(max(drawn.shape))
    spots = []
    for shift in (0, 1):
        where = [jax.random.randint(jax.random.fold_in(rng, axis), (), 0, length) for axis, length in enumerate(drawn.shape)]
        where[longest] = (where[longest] + shift) % drawn.shape[longest]
        spots.append(tuple(where))
    return drawn.at[spots[0]].set(smallest).at[spots[1]].set(top_value)


def levels(own_key, shape, split, low, top_value):
    loudness = 1.0
    for dim, shards_of in split:
        steps = jax.random.uniform(jax.random.fold_in(jax.random.fold_in(own_key, 6), dim), (shards_of,), jnp.float32, low / len(split), top_value / len(split))
        loudness = loudness * jnp.repeat(jnp.exp(steps), shape[dim] // shards_of).reshape((-1,) + (1,) * (len(shape) - 1 - dim))
    return loudness


def gaussian(own_key, shape, width, bound, shards=(), dtype=jnp.bfloat16):
    entries = jax.random.normal(own_key, shape, jnp.float32) * width
    if len(shards) > 0:
        entries = levels(own_key, shape, shards, -0.22, 0.18) * entries
    return jnp.clip(entries, min=-bound, max=bound).astype(dtype)


def setup_inputs(seed: int = 0) -> dict:
    arg_keys = jax.random.split(jax.random.key(seed), 8)
    hidden_in = gaussian(arg_keys[0], (SEQ, D), 1.0, 6.0, ((0, 128),))
    hidden_tan = gaussian(arg_keys[1], (SEQ, D), 1.0, 6.0, ((0, 128),))
    qkv_weight = gaussian(arg_keys[2], (3, D, HW), D ** -0.5, 0.125, ((2, 4),))
    out_weight = gaussian(arg_keys[3], (HW, D), HW ** -0.5, 0.1875, ((0, 4),))
    norm_gain = draw_norm_gain(jax.random.fold_in(arg_keys[7], 71), 0)
    pos_local = place_ends(jax.random.randint(arg_keys[5], (2, SEQ), 0, TILE), jax.random.fold_in(arg_keys[5], 1), 0, TILE - 1).astype(jnp.int32)
    tile_anchor = place_ends(jax.random.randint(arg_keys[6], (2, N_CTX), 0, 4 * TILE), jax.random.fold_in(arg_keys[6], 1), 0, (4 * TILE) - 1).astype(jnp.int32)
    return dict(hidden_in=hidden_in, hidden_tan=hidden_tan, qkv_weight=qkv_weight, out_weight=out_weight, norm_gain=norm_gain, pos_local=pos_local, tile_anchor=tile_anchor)


THETA = 10000.0

def angle_tables(position, head_size):
    quarter = head_size // 4
    frequency = THETA ** (-jnp.arange(quarter).astype(jnp.float32) / quarter)
    rows_angle = position[0].astype(jnp.float32)[:, None] * frequency
    cols_angle = position[1].astype(jnp.float32)[:, None] * frequency
    angles = jnp.concatenate([rows_angle, rows_angle, cols_angle, cols_angle], 1)
    return (jnp.cos(angles), jnp.sin(angles))

def rotate_heads(values, position):
    head_size = values.shape[-1]
    cosine, sine_table = angle_tables(position, head_size)
    quarter = head_size // 4
    wide = lax.optimization_barrier(values).astype(jnp.float32)
    parts = [wide[..., i * quarter:(i + 1) * quarter] for i in range(4)]
    turned = jnp.concatenate([-parts[1], parts[0], -parts[3], parts[2]], -1)
    result = wide * cosine[:, None, :] + turned * sine_table[:, None, :]
    return result.astype(jnp.bfloat16)

def norm_pair(raw, tangent, gain):
    square_mean = lax.optimization_barrier(jnp.mean(raw * raw, -1, keepdims=True)) + 1e-06
    factor = lax.rsqrt(square_mean)
    normed = raw * factor * gain
    cross = lax.optimization_barrier(jnp.mean(raw * tangent, -1, keepdims=True))
    normed_tan = gain * factor * (tangent - raw * cross / square_mean)
    return (normed.astype(jnp.bfloat16), normed_tan.astype(jnp.bfloat16))

def attend(query, query_tan, keys, keys_tan, values, values_tan):
    scale = query.shape[-1] ** (-0.5)
    query32 = query.astype(jnp.float32)
    keys32 = keys.astype(jnp.float32)
    scores = jnp.einsum('thd,shd->ths', query32, keys32) * scale
    score_tan = (jnp.einsum('thd,shd->ths', query_tan.astype(jnp.float32), keys32) + jnp.einsum('thd,shd->ths', query32, keys_tan.astype(jnp.float32))) * scale
    peak = lax.optimization_barrier(jnp.max(scores, -1, keepdims=True))
    expon = jnp.exp(scores - peak)
    weighted = expon * score_tan
    totals = lax.optimization_barrier(jnp.sum(expon, -1))[..., None]
    slopes = lax.optimization_barrier(jnp.sum(weighted, -1))[..., None]
    expon16 = expon.astype(jnp.bfloat16).astype(jnp.float32)
    weighted16 = weighted.astype(jnp.bfloat16).astype(jnp.float32)
    values32 = values.astype(jnp.float32)
    accum_out = jnp.einsum('ths,shd->thd', expon16, values32)
    accum_tan = jnp.einsum('ths,shd->thd', expon16, values_tan.astype(jnp.float32))
    accum_mix = jnp.einsum('ths,shd->thd', weighted16, values32)
    result = accum_out / totals
    result_tan = (accum_tan + accum_mix) / totals - slopes / totals * result
    count = query.shape[0]
    return (result.astype(jnp.bfloat16).reshape(count, -1), result_tan.astype(jnp.bfloat16).reshape(count, -1))

def reference(hidden_in, hidden_tan, qkv_weight, out_weight, norm_gain, pos_local, tile_anchor):
    head_size = norm_gain.shape[1]
    position = pos_local + jnp.repeat(tile_anchor, TOK_DEV, axis=1)
    stacked = jnp.concatenate([hidden_in, hidden_tan], 0).astype(jnp.float32)
    projected = jnp.einsum('td,cdh->cth', stacked, qkv_weight.astype(jnp.float32))
    shaped = projected.reshape(3, 2, SEQ, -1, head_size)
    query_n, query_tn = norm_pair(shaped[0, 0], shaped[0, 1], norm_gain[0])
    keys_n, keys_tn = norm_pair(shaped[1, 0], shaped[1, 1], norm_gain[1])
    values = shaped[2, 0].astype(jnp.bfloat16)
    values_tan = shaped[2, 1].astype(jnp.bfloat16)
    query = rotate_heads(query_n, position)
    query_tan = rotate_heads(query_tn, position)
    keys = rotate_heads(keys_n, position)
    keys_tan = rotate_heads(keys_tn, position)
    heads = query.shape[1]
    blocks_q = query.reshape(N_CTX, TOK_DEV, heads, head_size)
    blocks_t = query_tan.reshape(N_CTX, TOK_DEV, heads, head_size)

    def one_block(pair):
        return attend(pair[0], pair[1], keys, keys_tan, values, values_tan)
    result, result_tan = lax.map(one_block, (blocks_q, blocks_t))
    result = result.reshape(SEQ, -1)
    result_tan = result_tan.reshape(SEQ, -1)
    attention_out = jnp.dot(result, out_weight, preferred_element_type=jnp.float32).astype(jnp.bfloat16)
    attention_tan = jnp.dot(result_tan, out_weight, preferred_element_type=jnp.float32).astype(jnp.bfloat16)
    return (attention_out, attention_tan)
```

```python
import numpy as np
import jax
import jax.numpy as jnp
from jax import lax
from jax.experimental import pallas as pl
from jax.experimental.pallas import tpu as pltpu
from jax.sharding import PartitionSpec as P

THETA = 10000.0
MESH = pl.DeviceIdType.MESH
BF = jnp.bfloat16
F32 = jnp.float32

TOK = 32
HD = 128
NX, NY, NZ, NT = 4, 8, 2, 4
ROWS = NY * 2 * TOK
QB = 128
SCALE = HD**-0.5

XZ = [(2, 1), (1, 1), (3, 1), (2, 0), (1, 0), (3, 0), (0, 1), (0, 0)]
YS = [4, 3, 5, 2, 6, 1, 7, 0]


def slot_xz(dx, dz):
    return (dx % NX) * NZ + dz % NZ


def sin_cos(x):
    k = jnp.floor(x * 0.6366197723675814 + 0.5)
    r = ((x - k * 1.5703125) - k * 4.837512969970703125e-4) - k * 7.54978995489188216e-8
    r2 = r * r
    s = r + r * r2 * (-1.6666654611e-1 + r2 * (8.3321608736e-3 + r2 * -1.9515295891e-4))
    c = 1.0 - 0.5 * r2 + r2 * r2 * (
        4.166664568298827e-2 + r2 * (-1.388731625493765e-3 + r2 * 2.443315711809948e-5)
    )
    quad = k - 4.0 * jnp.floor(k * 0.25)
    odd = (quad == 1.0) | (quad == 3.0)
    sin = jnp.where(odd, c, s)
    cos = jnp.where(odd, s, c)
    sin = jnp.where(quad >= 2.0, -sin, sin)
    cos = jnp.where((quad == 1.0) | (quad == 2.0), -cos, cos)
    return sin, cos


def kernel(
    hin, htan, wqkv, wout, gain, pos, anchor, freq,
    out_a, out_t,
    h, w, wo, gain_v, pos_v, anchor_v, freq_v,
    kmsg, qmsg, vmsg, kbuf, qbuf, vbuf, part, stat, pbuf, sbuf, obuf,
    loc, ksend, krecv, qsend, qrecv, vsend, vrecv, psend, precv, ssend, srecv, osend, orecv,
    wsend, wrecv, fsend, frecv,
):
    ctx = lax.axis_index("ctx")
    tp = lax.axis_index("tp")
    z, x, y, core = ctx // 64, (ctx // 16) % NX, (ctx // 2) % NY, ctx % 2

    def chip_xz(dx, dz, c):
        return {"ctx": ((((z + dz) % NZ) * NX + (x + dx) % NX) * NY + y) * 2 + c}

    def chip_y(dy, c):
        return {"ctx": ((z * NX + x) * NY + (y + dy) % NY) * 2 + c}

    def peer_tp(dt):
        return {"tp": (tp + dt) % NT}

    other = 1 - core
    sibling = {"ctx": ctx + 1 - 2 * core}

    def fetch(i, src, dst):
        copy = pltpu.make_async_copy(src, dst, loc.at[i])
        copy.start()
        return copy

    get_pos = fetch(0, pos, pos_v)
    get_anchor = fetch(1, anchor, anchor_v)
    get_freq = fetch(2, freq, freq_v)
    get_hin = fetch(3, hin, h.at[pl.ds(0, TOK)])
    get_htan = fetch(4, htan, h.at[pl.ds(TOK, TOK)])
    get_wk = fetch(5, wqkv.at[1], w.at[1])
    get_gain = fetch(6, gain, gain_v)
    get_wq = fetch(7, wqkv.at[0], w.at[0])
    get_wv = fetch(8, wqkv.at[2], w.at[2])
    columns = NT * HD
    get_wo = fetch(9, wout.at[:, pl.ds(pl.multiple_of(tp * columns, columns), columns)], wo.at[0])

    barrier = pltpu.get_barrier_semaphore()
    count = 0
    for c in range(2):
        for dy in YS[:-1]:
            pl.semaphore_signal(barrier, inc=1, device_id=chip_y(dy, c), device_id_type=MESH)
            count += 1
        for dx, dz in XZ[:-1]:
            pl.semaphore_signal(barrier, inc=1, device_id=chip_xz(dx, dz, c), device_id_type=MESH)
            count += 1
    for dt in (1, 2, 3):
        pl.semaphore_signal(barrier, inc=1, device_id=peer_tp(dt), device_id_type=MESH)
        count += 1
    pl.semaphore_signal(barrier, inc=1, device_id=sibling, device_id_type=MESH)
    count += 1

    get_pos.wait()
    get_anchor.wait()
    get_freq.wait()
    place = (pos_v[...] + anchor_v[...]).astype(F32)
    eye = lax.broadcasted_iota(jnp.int32, (TOK, TOK), 0) == lax.broadcasted_iota(
        jnp.int32, (TOK, TOK), 1
    )
    row_id = jnp.sum(jnp.where(eye, place[0:1, :], 0.0), axis=1, keepdims=True)
    col_id = jnp.sum(jnp.where(eye, place[1:2, :], 0.0), axis=1, keepdims=True)
    lane = lax.broadcasted_iota(jnp.int32, (TOK, HD), 1)
    sine, cosine = sin_cos(jnp.where(lane < HD // 2, row_id, col_id) * freq_v[0:1, :])
    low = lane % (HD // 2) < HD // 4
    sine = jnp.where(low, -sine, sine)

    def rotate(n):
        wide = n.astype(BF).astype(F32)
        turned = jnp.where(low, pltpu.roll(wide, HD - HD // 4, 1), pltpu.roll(wide, HD // 4, 1))
        return (wide * cosine + turned * sine).astype(BF)

    def norm_rotate(projected, row, head):
        g = gain_v[row : row + 1, :]
        raw = projected[:TOK, head * HD : (head + 1) * HD]
        tan = projected[TOK:, head * HD : (head + 1) * HD]
        ms = jnp.mean(raw * raw, axis=1, keepdims=True) + 1e-06
        r = lax.rsqrt(ms)
        cross = jnp.mean(raw * tan, axis=1, keepdims=True)
        n = raw * r * g
        dn = g * r * (tan - raw * (cross / ms))
        return rotate(n), rotate(dn)

    def project(which):
        return jnp.dot(h[...], w[which], preferred_element_type=F32)

    def own_rows(slot):
        return pl.ds(pl.multiple_of(slot * 2 * TOK + core * TOK, TOK), TOK)

    def send(src, dst, ssem, rsem, device):
        copy = pltpu.make_async_remote_copy(
            src_ref=src, dst_ref=dst, send_sem=ssem, recv_sem=rsem,
            device_id=device, device_id_type=MESH,
        )
        copy.start()

    def spread_xz(msg, buf, ssem, rsem):
        for dx, dz in XZ:
            there = slot_xz(-dx, -dz)
            for flip in range(2):
                if (dx, dz) == (0, 0) and flip == 0:
                    continue
                c = core if flip == 0 else other
                send(
                    msg.at[c], buf.at[own_rows(there)],
                    ssem.at[there, flip], rsem.at[there, flip], chip_xz(dx, dz, c),
                )

    def spread_y(msg, buf, ssem, rsem):
        for dy in YS:
            there = (NY - dy) % NY
            for flip in range(2):
                if dy == 0 and flip == 0:
                    continue
                c = core if flip == 0 else other
                send(
                    msg.at[c], buf.at[own_rows(there)],
                    ssem.at[there, flip], rsem.at[there, flip], chip_y(dy, c),
                )

    def keep(msg, buf):
        buf[own_rows(0), :] = msg[core]

    def wait_bytes(ref, sem):
        pltpu.make_async_copy(ref, ref, sem).wait()

    def wait_slot(buf, sems, slot):
        for flip in range(2):
            if slot == 0 and flip == 0:
                continue
            wait_bytes(buf.at[pl.ds(0, TOK)], sems.at[slot, flip])

    get_gain.wait()
    get_hin.wait()
    get_htan.wait()
    get_wk.wait()
    projected = project(1)
    for head in range(2):
        k, dk = norm_rotate(projected, 1, head)
        kmsg[head, :, :HD] = k
        kmsg[head, :, HD:] = dk
    pl.semaphore_wait(barrier, count)
    spread_xz(kmsg, kbuf, ksend, krecv)
    get_wq.wait()
    projected = project(0)
    for head in range(2):
        q, dq = norm_rotate(projected, 0, head)
        qmsg[head, :, :HD] = dq
        qmsg[head, :, HD:] = q
    spread_y(qmsg, qbuf, qsend, qrecv)
    get_wv.wait()
    projected = project(2)
    for head in range(2):
        vmsg[head, :, :HD] = projected[:TOK, head * HD : (head + 1) * HD].astype(BF)
        vmsg[head, :, HD:] = projected[TOK:, head * HD : (head + 1) * HD].astype(BF)
    spread_xz(vmsg, vbuf, vsend, vrecv)
    keep(kmsg, kbuf)
    keep(qmsg, qbuf)
    keep(vmsg, vbuf)

    for slot in range(NX * NZ):
        wait_slot(kbuf, krecv, slot)
    for slot in range(NY):
        wait_slot(qbuf, qrecv, slot)
    for slot in range(NX * NZ):
        wait_slot(vbuf, vrecv, slot)

    half = pl.ds(pl.multiple_of(core * HD, HD), HD)
    for dt in (2, 1, 3):
        to = (tp + dt) % NT
        send(
            wout.at[half, pl.ds(pl.multiple_of(to * columns, columns), columns)],
            wo.at[NT - dt, half], wsend.at[dt], wrecv.at[NT - dt], peer_tp(dt),
        )

    nt = (((1,), (1,)), ((), ()))
    blocks = ROWS // QB
    lane_s = lax.broadcasted_iota(jnp.int32, (QB, HD), 1)
    for b in (2, 1, 3, 0):
        rows = pl.ds(b * QB, QB)
        s = lax.dot_general(qbuf[rows, HD:], kbuf[:, :HD], nt, preferred_element_type=F32) * SCALE
        ds = lax.dot_general(qbuf[rows, :], kbuf[...], nt, preferred_element_type=F32) * SCALE
        m = jnp.max(s, axis=1, keepdims=True)
        e = jnp.exp(s - m)
        weighted = e * ds
        l = jnp.sum(e, axis=1, keepdims=True)
        g = jnp.sum(weighted, axis=1, keepdims=True)
        both = jnp.dot(e.astype(BF), vbuf[...], preferred_element_type=F32)
        mix = jnp.dot(weighted.astype(BF), vbuf[:, :HD], preferred_element_type=F32)
        inv = 1.0 / l
        slope = g * inv
        o = both[:, :HD] * inv
        part[rows, :HD] = o.astype(BF)
        part[rows, HD:] = ((both[:, HD:] + mix) * inv - slope * o).astype(BF)
        packed = jnp.where(lane_s == 0, m, jnp.where(lane_s == 1, l, jnp.where(lane_s == 2, slope, 0.0)))
        stat[b] = packed.T[:8, :]
        for dy in (2 * b, 2 * b + 1):
            there = (NY - dy) % NY
            for flip in range(2):
                if dy == 0 and flip == 0:
                    continue
                c = core if flip == 0 else other
                src = pl.ds(pl.multiple_of(dy * 2 * TOK + c * TOK, TOK), TOK)
                send(
                    stat.at[b], sbuf.at[core, there],
                    ssend.at[there, flip], srecv.at[there, flip], chip_y(dy, c),
                )
                send(
                    part.at[src], pbuf.at[core, there],
                    psend.at[there, flip], precv.at[there, flip], chip_y(dy, c),
                )
    pbuf[core, 0] = part[pl.ds(pl.multiple_of(core * TOK, TOK), TOK), :]
    sbuf[core, 0] = stat[0]

    for slot in range(NX * NZ):
        wait_slot(kbuf, ksend, slot)
        wait_slot(qbuf, qsend, slot)
        wait_slot(vbuf, vsend, slot)

    for slot in range(NY):
        for flip in range(2):
            if slot == 0 and flip == 0:
                continue
            wait_bytes(sbuf.at[0, 0], srecv.at[slot, flip])
    coefs = []
    for head in range(2):
        rows_of = []
        for kind in range(3):
            line = jnp.concatenate([sbuf[head, slot, kind : kind + 1, :] for slot in range(NY)], 0)
            rows_of.append(line)
        odd = lax.broadcasted_iota(jnp.int32, (NY, HD), 0) % 2 == 1
        aligned = []
        for line in rows_of:
            line = jnp.where(odd, pltpu.roll(line, HD // 2, 1), line)
            aligned.append(jnp.where(core == 1, pltpu.roll(line, HD - TOK, 1), line))
        m, l, slope = aligned
        top = jnp.max(m, axis=0, keepdims=True)
        weight = jnp.exp(m - top) * l
        weight = weight / jnp.sum(weight, axis=0, keepdims=True)
        mean_slope = jnp.sum(weight * slope, axis=0, keepdims=True)
        coefs += [weight, weight * (slope - mean_slope)]
    coefs.append(jnp.zeros((HD - 4 * NY, HD), F32))
    table = jnp.concatenate(coefs, 0).T[:TOK, :]
    for slot in range(NY):
        for flip in range(2):
            if slot == 0 and flip == 0:
                continue
            wait_bytes(pbuf.at[0, 0], precv.at[slot, flip])
    for head in range(2):
        o = jnp.zeros((TOK, HD), F32)
        do = jnp.zeros((TOK, HD), F32)
        for slot in range(NY):
            at = head * 2 * NY + slot
            a = table[:, at : at + 1]
            b = table[:, at + NY : at + NY + 1]
            value = pbuf[head, slot, :, :HD].astype(F32)
            o += a * value
            do += a * pbuf[head, slot, :, HD:].astype(F32) + b * value
        obuf[0, :TOK, head * HD : (head + 1) * HD] = o.astype(BF)
        obuf[0, TOK:, head * HD : (head + 1) * HD] = do.astype(BF)
    for dt in (2, 1, 3):
        send(obuf.at[0], obuf.at[NT - dt], osend.at[dt], orecv.at[NT - dt], peer_tp(dt))

    for dt in (1, 3, 2):
        wait_bytes(wo.at[0, pl.ds(0, HD)], wrecv.at[dt])
        send(wo.at[dt, half], wo.at[dt, half], fsend.at[dt], frecv.at[dt], sibling)
    for slot in range(NY):
        for flip in range(2):
            if slot == 0 and flip == 0:
                continue
            wait_bytes(sbuf.at[0, 0], ssend.at[slot, flip])
            wait_bytes(pbuf.at[0, 0], psend.at[slot, flip])
    get_wo.wait()
    total = jnp.dot(obuf[0], wo[0], preferred_element_type=F32)
    for dt in (1, 3, 2):
        wait_bytes(wo.at[0, pl.ds(0, HD)], frecv.at[dt])
        wait_bytes(obuf.at[0], orecv.at[dt])
        total += jnp.dot(obuf[dt], wo[dt], preferred_element_type=F32)
    out_a[...] = total[:TOK].astype(BF)
    out_t[...] = total[TOK:].astype(BF)
    for dt in (1, 2, 3):
        wait_bytes(wo.at[0, pl.ds(0, HD)], wsend.at[dt])
        wait_bytes(wo.at[0, pl.ds(0, HD)], fsend.at[dt])
        wait_bytes(obuf.at[0], osend.at[dt])


def on_device(hidden_in, hidden_tan, qkv_weight, out_weight, norm_gain, pos_local, tile_anchor):
    quarter = HD // 4
    frequency = np.float32(THETA) ** (-np.arange(quarter, dtype=np.float32) / np.float32(quarter))
    freq = jnp.asarray(np.tile(frequency.astype(np.float32), (8, 4)))
    anywhere = pl.BlockSpec(memory_space=pl.ANY)
    vmem = pl.BlockSpec(memory_space=pltpu.VMEM)
    dma = pltpu.SemaphoreType.DMA
    columns = NT * HD
    out = jax.ShapeDtypeStruct((TOK, columns), BF)
    return pl.pallas_call(
        kernel,
        out_shape=(out, out),
        in_specs=[anywhere] * 8,
        out_specs=(vmem, vmem),
        scratch_shapes=[
            pltpu.VMEM((2 * TOK, 2048), BF),
            pltpu.VMEM((3, 2048, 2 * HD), BF),
            pltpu.VMEM((NT, 2 * HD, columns), BF),
            pltpu.VMEM((2, HD), F32),
            pltpu.VMEM((2, TOK), jnp.int32),
            pltpu.VMEM((2, 1), jnp.int32),
            pltpu.VMEM((8, HD), F32),
            pltpu.VMEM((2, TOK, 2 * HD), BF),
            pltpu.VMEM((2, TOK, 2 * HD), BF),
            pltpu.VMEM((2, TOK, 2 * HD), BF),
            pltpu.VMEM((ROWS, 2 * HD), BF),
            pltpu.VMEM((ROWS, 2 * HD), BF),
            pltpu.VMEM((ROWS, 2 * HD), BF),
            pltpu.VMEM((ROWS, 2 * HD), BF),
            pltpu.VMEM((ROWS // QB, 8, HD), F32),
            pltpu.VMEM((2, NY, TOK, 2 * HD), BF),
            pltpu.VMEM((2, NY, 8, HD), F32),
            pltpu.VMEM((NT, 2 * TOK, 2 * HD), BF),
            dma((10,)),
        ]
        + [dma((8, 2))] * 10
        + [dma((NT,))] * 6,
        compiler_params=pltpu.CompilerParams(
            collective_id=0, has_side_effects=True, vmem_limit_bytes=40 * 2**20
        ),
    )(hidden_in, hidden_tan, qkv_weight, out_weight, norm_gain, pos_local, tile_anchor, freq)


def solution(mesh):
    in_specs = (
        P("ctx", None),
        P("ctx", None),
        P(None, None, "tp"),
        P("tp", None),
        P(),
        P(None, "ctx"),
        P(None, "ctx"),
    )
    out_specs = (P("ctx", "tp"), P("ctx", "tp"))
    return jax.shard_map(
        on_device, mesh=mesh, in_specs=in_specs, out_specs=out_specs, check_vma=False
    )
```

```python
import numpy as np
import jax
import jax.numpy as jnp
from jax import lax
from jax.experimental import pallas as pl
from jax.experimental.pallas import tpu as pltpu
from jax.sharding import PartitionSpec as P

THETA = 10000.0
MESH = pl.DeviceIdType.MESH
BF = jnp.bfloat16
F32 = jnp.float32

TOK = 32
HD = 128
NX, NY, NZ, NT = 4, 8, 2, 4
ROWS = NY * 2 * TOK
QB = 128
SCALE = HD**-0.5

XZ = [(2, 1), (1, 1), (3, 1), (2, 0), (1, 0), (3, 0), (0, 1), (0, 0)]
YS = [4, 3, 5, 2, 6, 1, 7, 0]


def slot_xz(dx, dz):
    return (dx % NX) * NZ + dz % NZ


def sin_cos(x):
    k = jnp.floor(x * 0.6366197723675814 + 0.5)
    r = ((x - k * 1.5703125) - k * 4.837512969970703125e-4) - k * 7.54978995489188216e-8
    r2 = r * r
    s = r + r * r2 * (-1.6666654611e-1 + r2 * (8.3321608736e-3 + r2 * -1.9515295891e-4))
    c = 1.0 - 0.5 * r2 + r2 * r2 * (
        4.166664568298827e-2 + r2 * (-1.388731625493765e-3 + r2 * 2.443315711809948e-5)
    )
    quad = k - 4.0 * jnp.floor(k * 0.25)
    odd = (quad == 1.0) | (quad == 3.0)
    sin = jnp.where(odd, c, s)
    cos = jnp.where(odd, s, c)
    sin = jnp.where(quad >= 2.0, -sin, sin)
    cos = jnp.where((quad == 1.0) | (quad == 2.0), -cos, cos)
    return sin, cos


def kernel(
    hin, htan, wqkv, wout, gain, pos, anchor, freq,
    out,
    h, w, wo, gain_v, pos_v, anchor_v, freq_v,
    kmsg, qmsg, vmsg, kbuf, qbuf, vbuf, part, stat, pbuf, sbuf, obuf,
    loc, ksend, krecv, qsend, qrecv, vsend, vrecv, psend, precv, ssend, srecv, osend, orecv,
    wsend, wrecv, fsend, frecv,
):
    ctx = lax.axis_index("ctx")
    tp = lax.axis_index("tp")
    z, x, y, core = ctx // 64, (ctx // 16) % NX, (ctx // 2) % NY, ctx % 2

    def chip_xz(dx, dz, c):
        return {"ctx": ((((z + dz) % NZ) * NX + (x + dx) % NX) * NY + y) * 2 + c}

    def chip_y(dy, c):
        return {"ctx": ((z * NX + x) * NY + (y + dy) % NY) * 2 + c}

    def peer_tp(dt):
        return {"tp": (tp + dt) % NT}

    other = 1 - core
    sibling = {"ctx": ctx + 1 - 2 * core}

    barrier = pltpu.get_barrier_semaphore()
    count = 0
    for c in range(2):
        for dy in YS[:-1]:
            pl.semaphore_signal(barrier, inc=1, device_id=chip_y(dy, c), device_id_type=MESH)
            count += 1
        for dx, dz in XZ[:-1]:
            pl.semaphore_signal(barrier, inc=1, device_id=chip_xz(dx, dz, c), device_id_type=MESH)
            count += 1
    for dt in (1, 2, 3):
        pl.semaphore_signal(barrier, inc=1, device_id=peer_tp(dt), device_id_type=MESH)
        count += 1
    pl.semaphore_signal(barrier, inc=1, device_id=sibling, device_id_type=MESH)
    count += 1

    def fetch(i, src, dst):
        copy = pltpu.make_async_copy(src, dst, loc.at[i])
        copy.start()
        return copy

    get_pos = fetch(0, pos, pos_v)
    get_anchor = fetch(1, anchor, anchor_v)
    get_freq = fetch(2, freq, freq_v)
    get_hin = fetch(3, hin, h.at[pl.ds(0, TOK)])
    get_htan = fetch(4, htan, h.at[pl.ds(TOK, TOK)])
    get_wk = fetch(5, wqkv.at[1], w.at[1])
    get_gain = fetch(6, gain, gain_v)
    get_wq = fetch(7, wqkv.at[0], w.at[0])
    get_wv = fetch(8, wqkv.at[2], w.at[2])
    columns = NT * HD
    get_wo = fetch(9, wout.at[:, pl.ds(pl.multiple_of(tp * columns, columns), columns)], wo.at[0])

    get_pos.wait()
    get_anchor.wait()
    get_freq.wait()
    row_place = pos_v[0:1, :] + anchor_v[:, 0:1]
    col_place = pos_v[1:2, :] + anchor_v[:, 1:2]
    eye = lax.broadcasted_iota(jnp.int32, (TOK, TOK), 0) == lax.broadcasted_iota(
        jnp.int32, (TOK, TOK), 1
    )
    row_id = jnp.sum(jnp.where(eye, row_place.astype(F32), 0.0), axis=1, keepdims=True)
    col_id = jnp.sum(jnp.where(eye, col_place.astype(F32), 0.0), axis=1, keepdims=True)
    lane = lax.broadcasted_iota(jnp.int32, (TOK, HD), 1)
    sine, cosine = sin_cos(jnp.where(lane < HD // 2, row_id, col_id) * freq_v[0:1, :])
    low = lane % (HD // 2) < HD // 4
    sine = jnp.where(low, -sine, sine)

    def rotate(n):
        wide = n.astype(BF).astype(F32)
        turned = jnp.where(low, pltpu.roll(wide, HD - HD // 4, 1), pltpu.roll(wide, HD // 4, 1))
        return (wide * cosine + turned * sine).astype(BF)

    def norm_rotate(projected, row, head):
        g = gain_v[row : row + 1, :]
        raw = projected[:TOK, head * HD : (head + 1) * HD]
        tan = projected[TOK:, head * HD : (head + 1) * HD]
        ms = jnp.mean(raw * raw, axis=1, keepdims=True) + 1e-06
        r = lax.rsqrt(ms)
        cross = jnp.mean(raw * tan, axis=1, keepdims=True)
        n = raw * r * g
        dn = g * r * (tan - raw * (cross / ms))
        return rotate(n), rotate(dn)

    def project(which):
        return jnp.dot(h[...], w[which], preferred_element_type=F32)

    def own_rows(slot):
        return pl.ds(pl.multiple_of(slot * 2 * TOK + core * TOK, TOK), TOK)

    def send(src, dst, ssem, rsem, device):
        copy = pltpu.make_async_remote_copy(
            src_ref=src, dst_ref=dst, send_sem=ssem, recv_sem=rsem,
            device_id=device, device_id_type=MESH,
        )
        copy.start()

    def spread_xz(msg, buf, ssem, rsem):
        for dx, dz in XZ:
            there = slot_xz(-dx, -dz)
            for flip in range(2):
                if (dx, dz) == (0, 0) and flip == 0:
                    continue
                c = core if flip == 0 else other
                send(
                    msg.at[c], buf.at[own_rows(there)],
                    ssem.at[there, flip], rsem.at[there, flip], chip_xz(dx, dz, c),
                )

    def spread_y(msg, buf, ssem, rsem):
        for dy in YS:
            there = (NY - dy) % NY
            for flip in range(2):
                if dy == 0 and flip == 0:
                    continue
                c = core if flip == 0 else other
                send(
                    msg.at[c], buf.at[own_rows(there)],
                    ssem.at[there, flip], rsem.at[there, flip], chip_y(dy, c),
                )

    def keep(msg, buf):
        buf[own_rows(0), :] = msg[core]

    def wait_bytes(ref, sem):
        pltpu.make_async_copy(ref, ref, sem).wait()

    def wait_slot(buf, sems, slot):
        for flip in range(2):
            if slot == 0 and flip == 0:
                continue
            wait_bytes(buf.at[pl.ds(0, TOK)], sems.at[slot, flip])

    get_gain.wait()
    get_hin.wait()
    get_htan.wait()
    get_wk.wait()
    projected = project(1)
    for head in range(2):
        k, dk = norm_rotate(projected, 1, head)
        kmsg[head, :, :HD] = k
        kmsg[head, :, HD:] = dk
    pl.semaphore_wait(barrier, count)
    spread_xz(kmsg, kbuf, ksend, krecv)
    get_wq.wait()
    projected = project(0)
    for head in range(2):
        q, dq = norm_rotate(projected, 0, head)
        qmsg[head, :, :HD] = dq
        qmsg[head, :, HD:] = q
    spread_y(qmsg, qbuf, qsend, qrecv)
    get_wv.wait()
    projected = project(2)
    for head in range(2):
        vmsg[head, :, :HD] = projected[:TOK, head * HD : (head + 1) * HD].astype(BF)
        vmsg[head, :, HD:] = projected[TOK:, head * HD : (head + 1) * HD].astype(BF)
    spread_xz(vmsg, vbuf, vsend, vrecv)
    keep(kmsg, kbuf)
    keep(qmsg, qbuf)
    keep(vmsg, vbuf)

    for slot in range(NX * NZ):
        wait_slot(kbuf, krecv, slot)
    for slot in range(NY):
        wait_slot(qbuf, qrecv, slot)
    for slot in range(NX * NZ):
        wait_slot(vbuf, vrecv, slot)

    half = pl.ds(pl.multiple_of(core * HD, HD), HD)
    for dt in (2, 1, 3):
        to = (tp + dt) % NT
        send(
            wout.at[half, pl.ds(pl.multiple_of(to * columns, columns), columns)],
            wo.at[NT - dt, half], wsend.at[dt], wrecv.at[NT - dt], peer_tp(dt),
        )

    nt = (((1,), (1,)), ((), ()))
    blocks = ROWS // QB
    lane_s = lax.broadcasted_iota(jnp.int32, (QB, HD), 1)
    for b in (2, 1, 3, 0):
        rows = pl.ds(b * QB, QB)
        s = lax.dot_general(qbuf[rows, HD:], kbuf[:, :HD], nt, preferred_element_type=F32) * SCALE
        ds = lax.dot_general(qbuf[rows, :], kbuf[...], nt, preferred_element_type=F32) * SCALE
        m = jnp.max(s, axis=1, keepdims=True)
        e = jnp.exp(s - m)
        weighted = e * ds
        l = jnp.sum(e, axis=1, keepdims=True)
        g = jnp.sum(weighted, axis=1, keepdims=True)
        both = jnp.dot(e.astype(BF), vbuf[...], preferred_element_type=F32)
        mix = jnp.dot(weighted.astype(BF), vbuf[:, :HD], preferred_element_type=F32)
        inv = 1.0 / l
        slope = g * inv
        o = both[:, :HD] * inv
        part[rows, :HD] = o.astype(BF)
        part[rows, HD:] = ((both[:, HD:] + mix) * inv - slope * o).astype(BF)
        packed = jnp.where(lane_s == 0, m, jnp.where(lane_s == 1, l, jnp.where(lane_s == 2, slope, 0.0)))
        stat[b] = packed.T[:8, :]
        for dy in (2 * b, 2 * b + 1):
            there = (NY - dy) % NY
            for flip in range(2):
                if dy == 0 and flip == 0:
                    continue
                c = core if flip == 0 else other
                src = pl.ds(pl.multiple_of(dy * 2 * TOK + c * TOK, TOK), TOK)
                send(
                    stat.at[b], sbuf.at[core, there],
                    ssend.at[there, flip], srecv.at[there, flip], chip_y(dy, c),
                )
                send(
                    part.at[src], pbuf.at[core, there],
                    psend.at[there, flip], precv.at[there, flip], chip_y(dy, c),
                )
    pbuf[core, 0] = part[pl.ds(pl.multiple_of(core * TOK, TOK), TOK), :]
    sbuf[core, 0] = stat[0]

    for slot in range(NX * NZ):
        wait_slot(kbuf, ksend, slot)
        wait_slot(qbuf, qsend, slot)
        wait_slot(vbuf, vsend, slot)

    for slot in range(NY):
        for flip in range(2):
            if slot == 0 and flip == 0:
                continue
            wait_bytes(sbuf.at[0, 0], srecv.at[slot, flip])
    coefs = []
    for head in range(2):
        rows_of = []
        for kind in range(3):
            line = jnp.concatenate([sbuf[head, slot, kind : kind + 1, :] for slot in range(NY)], 0)
            rows_of.append(line)
        odd = lax.broadcasted_iota(jnp.int32, (NY, HD), 0) % 2 == 1
        aligned = []
        for line in rows_of:
            line = jnp.where(odd, pltpu.roll(line, HD // 2, 1), line)
            aligned.append(jnp.where(core == 1, pltpu.roll(line, HD - TOK, 1), line))
        m, l, slope = aligned
        top = jnp.max(m, axis=0, keepdims=True)
        weight = jnp.exp(m - top) * l
        weight = weight / jnp.sum(weight, axis=0, keepdims=True)
        mean_slope = jnp.sum(weight * slope, axis=0, keepdims=True)
        coefs += [weight, weight * (slope - mean_slope)]
    coefs.append(jnp.zeros((HD - 4 * NY, HD), F32))
    table = jnp.concatenate(coefs, 0).T[:TOK, :]
    for slot in range(NY):
        for flip in range(2):
            if slot == 0 and flip == 0:
                continue
            wait_bytes(pbuf.at[0, 0], precv.at[slot, flip])
    for head in range(2):
        o = jnp.zeros((TOK, HD), F32)
        do = jnp.zeros((TOK, HD), F32)
        for slot in range(NY):
            at = head * 2 * NY + slot
            a = table[:, at : at + 1]
            b = table[:, at + NY : at + NY + 1]
            value = pbuf[head, slot, :, :HD].astype(F32)
            o += a * value
            do += a * pbuf[head, slot, :, HD:].astype(F32) + b * value
        obuf[0, :TOK, head * HD : (head + 1) * HD] = o.astype(BF)
        obuf[0, TOK:, head * HD : (head + 1) * HD] = do.astype(BF)
    for dt in (2, 1, 3):
        send(obuf.at[0], obuf.at[NT - dt], osend.at[dt], orecv.at[NT - dt], peer_tp(dt))

    for dt in (1, 3, 2):
        wait_bytes(wo.at[0, pl.ds(0, HD)], wrecv.at[dt])
        send(wo.at[dt, half], wo.at[dt, half], fsend.at[dt], frecv.at[dt], sibling)
    for slot in range(NY):
        for flip in range(2):
            if slot == 0 and flip == 0:
                continue
            wait_bytes(sbuf.at[0, 0], ssend.at[slot, flip])
            wait_bytes(pbuf.at[0, 0], psend.at[slot, flip])
    get_wo.wait()
    total = jnp.dot(obuf[0], wo[0], preferred_element_type=F32)
    for dt in (1, 3, 2):
        wait_bytes(wo.at[0, pl.ds(0, HD)], frecv.at[dt])
        wait_bytes(obuf.at[0], orecv.at[dt])
        total += jnp.dot(obuf[dt], wo[dt], preferred_element_type=F32)
    out[...] = total.astype(BF)
    for dt in (1, 2, 3):
        wait_bytes(wo.at[0, pl.ds(0, HD)], wsend.at[dt])
        wait_bytes(wo.at[0, pl.ds(0, HD)], fsend.at[dt])
        wait_bytes(obuf.at[0], osend.at[dt])


def on_device(hidden_in, hidden_tan, qkv_weight, out_weight, norm_gain, pos_local, tile_anchor):
    quarter = HD // 4
    frequency = np.float32(THETA) ** (-np.arange(quarter, dtype=np.float32) / np.float32(quarter))
    freq = jnp.asarray(np.tile(frequency.astype(np.float32), (8, 4)))
    hbm = pl.BlockSpec(memory_space=pltpu.HBM)
    vmem = pl.BlockSpec(memory_space=pltpu.VMEM)
    dma = pltpu.SemaphoreType.DMA
    columns = NT * HD
    both = pl.pallas_call(
        kernel,
        out_shape=jax.ShapeDtypeStruct((2 * TOK, columns), BF),
        in_specs=[hbm] * 8,
        out_specs=vmem,
        scratch_shapes=[
            pltpu.VMEM((2 * TOK, 2048), BF),
            pltpu.VMEM((3, 2048, 2 * HD), BF),
            pltpu.VMEM((NT, 2 * HD, columns), BF),
            pltpu.VMEM((2, HD), F32),
            pltpu.VMEM((2, TOK), jnp.int32),
            pltpu.VMEM((1, 2), jnp.int32),
            pltpu.VMEM((8, HD), F32),
            pltpu.VMEM((2, TOK, 2 * HD), BF),
            pltpu.VMEM((2, TOK, 2 * HD), BF),
            pltpu.VMEM((2, TOK, 2 * HD), BF),
            pltpu.VMEM((ROWS, 2 * HD), BF),
            pltpu.VMEM((ROWS, 2 * HD), BF),
            pltpu.VMEM((ROWS, 2 * HD), BF),
            pltpu.VMEM((ROWS, 2 * HD), BF),
            pltpu.VMEM((ROWS // QB, 8, HD), F32),
            pltpu.VMEM((2, NY, TOK, 2 * HD), BF),
            pltpu.VMEM((2, NY, 8, HD), F32),
            pltpu.VMEM((NT, 2 * TOK, 2 * HD), BF),
            dma((10,)),
        ]
        + [dma((8, 2))] * 10
        + [dma((NT,))] * 6,
        compiler_params=pltpu.CompilerParams(
            collective_id=0, has_side_effects=True, vmem_limit_bytes=60 * 2**20
        ),
    )(hidden_in, hidden_tan, qkv_weight, out_weight, norm_gain, pos_local, tile_anchor.reshape(1, 2), freq)
    return both[:TOK], both[TOK:]


def solution(mesh):
    in_specs = (
        P("ctx", None),
        P("ctx", None),
        P(None, None, "tp"),
        P("tp", None),
        P(),
        P(None, "ctx"),
        P(None, "ctx"),
    )
    out_specs = (P("ctx", "tp"), P("ctx", "tp"))
    return jax.shard_map(
        on_device, mesh=mesh, in_specs=in_specs, out_specs=out_specs, check_vma=False
    )
```

```python
import numpy as np
import jax
import jax.numpy as jnp
from jax import lax
from jax.experimental import pallas as pl
from jax.experimental.pallas import tpu as pltpu
from jax.sharding import PartitionSpec as P

THETA = 10000.0
MESH = pl.DeviceIdType.MESH
BF = jnp.bfloat16
F32 = jnp.float32

TOK = 32
HD = 128
NX, NY, NZ, NT = 4, 8, 2, 4
ROWS = NY * 2 * TOK
QB = 128
SCALE = HD**-0.5

XZ = [(2, 1), (1, 1), (3, 1), (2, 0), (1, 0), (3, 0), (0, 1), (0, 0)]
YS = [4, 3, 5, 2, 6, 1, 7, 0]


def slot_xz(dx, dz):
    return (dx % NX) * NZ + dz % NZ


def sin_cos(x):
    k = jnp.floor(x * 0.6366197723675814 + 0.5)
    r = ((x - k * 1.5703125) - k * 4.837512969970703125e-4) - k * 7.54978995489188216e-8
    r2 = r * r
    s = r + r * r2 * (-1.6666654611e-1 + r2 * (8.3321608736e-3 + r2 * -1.9515295891e-4))
    c = 1.0 - 0.5 * r2 + r2 * r2 * (
        4.166664568298827e-2 + r2 * (-1.388731625493765e-3 + r2 * 2.443315711809948e-5)
    )
    quad = k - 4.0 * jnp.floor(k * 0.25)
    odd = (quad == 1.0) | (quad == 3.0)
    sin = jnp.where(odd, c, s)
    cos = jnp.where(odd, s, c)
    sin = jnp.where(quad >= 2.0, -sin, sin)
    cos = jnp.where((quad == 1.0) | (quad == 2.0), -cos, cos)
    return sin, cos


def kernel(
    hin, htan, wqkv, wout, gain, pos, anchor, freq,
    out,
    h, w, wo, gain_v, pos_v, anchor_v, freq_v,
    kmsg, qmsg, vmsg, kbuf, qbuf, vbuf, part, stat, pbuf, sbuf, obuf,
    loc, sent, recv, orecv,
):
    ctx = lax.axis_index("ctx")
    tp = lax.axis_index("tp")
    z, x, y, core = ctx // 64, (ctx // 16) % NX, (ctx // 2) % NY, ctx % 2

    def chip_xz(dx, dz, c):
        return {"ctx": ((((z + dz) % NZ) * NX + (x + dx) % NX) * NY + y) * 2 + c}

    def chip_y(dy, c):
        return {"ctx": ((z * NX + x) * NY + (y + dy) % NY) * 2 + c}

    def peer_tp(dt):
        return {"tp": (tp + dt) % NT}

    other = 1 - core
    sibling = {"ctx": ctx + 1 - 2 * core}

    barrier = pltpu.get_barrier_semaphore()
    count = 0
    for c in range(2):
        for dy in YS[:-1]:
            pl.semaphore_signal(barrier, inc=1, device_id=chip_y(dy, c), device_id_type=MESH)
            count += 1
        for dx, dz in XZ[:-1]:
            pl.semaphore_signal(barrier, inc=1, device_id=chip_xz(dx, dz, c), device_id_type=MESH)
            count += 1
    for dt in (1, 2, 3):
        pl.semaphore_signal(barrier, inc=1, device_id=peer_tp(dt), device_id_type=MESH)
        count += 1
    pl.semaphore_signal(barrier, inc=1, device_id=sibling, device_id_type=MESH)
    count += 1

    def fetch(i, src, dst):
        copy = pltpu.make_async_copy(src, dst, loc.at[i])
        copy.start()
        return copy

    get_pos = fetch(0, pos, pos_v)
    get_anchor = fetch(1, anchor, anchor_v)
    get_freq = fetch(2, freq, freq_v)
    get_hin = fetch(3, hin, h.at[pl.ds(0, TOK)])
    get_htan = fetch(4, htan, h.at[pl.ds(TOK, TOK)])
    get_wk = fetch(5, wqkv.at[1], w.at[1])
    get_gain = fetch(6, gain, gain_v)
    get_wq = fetch(7, wqkv.at[0], w.at[0])
    get_wv = fetch(8, wqkv.at[2], w.at[2])
    columns = NT * HD
    get_wo = fetch(9, wout.at[:, pl.ds(pl.multiple_of(tp * columns, columns), columns)], wo.at[0])

    get_pos.wait()
    get_anchor.wait()
    get_freq.wait()
    row_place = pos_v[0:1, :] + anchor_v[:, 0:1]
    col_place = pos_v[1:2, :] + anchor_v[:, 1:2]
    eye = lax.broadcasted_iota(jnp.int32, (TOK, TOK), 0) == lax.broadcasted_iota(
        jnp.int32, (TOK, TOK), 1
    )
    row_id = jnp.sum(jnp.where(eye, row_place.astype(F32), 0.0), axis=1, keepdims=True)
    col_id = jnp.sum(jnp.where(eye, col_place.astype(F32), 0.0), axis=1, keepdims=True)
    lane = lax.broadcasted_iota(jnp.int32, (TOK, HD), 1)
    sine, cosine = sin_cos(jnp.where(lane < HD // 2, row_id, col_id) * freq_v[0:1, :])
    low = lane % (HD // 2) < HD // 4
    sine = jnp.where(low, -sine, sine)

    def rotate(n):
        wide = n.astype(BF).astype(F32)
        turned = jnp.where(low, pltpu.roll(wide, HD - HD // 4, 1), pltpu.roll(wide, HD // 4, 1))
        return (wide * cosine + turned * sine).astype(BF)

    def norm_rotate(projected, row, head):
        g = gain_v[row : row + 1, :]
        raw = projected[:TOK, head * HD : (head + 1) * HD]
        tan = projected[TOK:, head * HD : (head + 1) * HD]
        ms = jnp.mean(raw * raw, axis=1, keepdims=True) + 1e-06
        r = lax.rsqrt(ms)
        cross = jnp.mean(raw * tan, axis=1, keepdims=True)
        n = raw * r * g
        dn = g * r * (tan - raw * (cross / ms))
        return rotate(n), rotate(dn)

    def project(which):
        return jnp.dot(h[...], w[which], preferred_element_type=F32)

    def own_rows(slot):
        return pl.ds(pl.multiple_of(slot * 2 * TOK + core * TOK, TOK), TOK)

    def send(src, dst, ssem, rsem, device):
        copy = pltpu.make_async_remote_copy(
            src_ref=src, dst_ref=dst, send_sem=ssem, recv_sem=rsem,
            device_id=device, device_id_type=MESH,
        )
        copy.start()

    def spread_xz(msg, buf, ssem, rsem):
        for dx, dz in XZ:
            there = slot_xz(-dx, -dz)
            for flip in range(2):
                if (dx, dz) == (0, 0) and flip == 0:
                    continue
                c = core if flip == 0 else other
                send(
                    msg.at[c], buf.at[own_rows(there)],
                    ssem, rsem, chip_xz(dx, dz, c),
                )

    def spread_y(msg, buf, ssem, rsem):
        for dy in YS:
            there = (NY - dy) % NY
            for flip in range(2):
                if dy == 0 and flip == 0:
                    continue
                c = core if flip == 0 else other
                send(
                    msg.at[c], buf.at[own_rows(there)],
                    ssem, rsem, chip_y(dy, c),
                )

    def keep(msg, buf):
        buf[own_rows(0), :] = msg[core]

    def wait_bytes(ref, sem):
        pltpu.make_async_copy(ref, ref, sem).wait()

    peers = 2 * NY - 1

    def wait_all(buf, sem):
        wait_bytes(buf.at[pl.ds(0, peers * TOK)], sem)

    get_gain.wait()
    get_hin.wait()
    get_htan.wait()
    get_wk.wait()
    projected = project(1)
    for head in range(2):
        k, dk = norm_rotate(projected, 1, head)
        kmsg[head, :, :HD] = k
        kmsg[head, :, HD:] = dk
    pl.semaphore_wait(barrier, count)
    spread_xz(kmsg, kbuf, sent.at[0], recv.at[0])
    get_wq.wait()
    projected = project(0)
    for head in range(2):
        q, dq = norm_rotate(projected, 0, head)
        qmsg[head, :, :HD] = dq
        qmsg[head, :, HD:] = q
    spread_y(qmsg, qbuf, sent.at[1], recv.at[1])
    get_wv.wait()
    projected = project(2)
    for head in range(2):
        vmsg[head, :, :HD] = projected[:TOK, head * HD : (head + 1) * HD].astype(BF)
        vmsg[head, :, HD:] = projected[TOK:, head * HD : (head + 1) * HD].astype(BF)
    spread_xz(vmsg, vbuf, sent.at[2], recv.at[2])
    keep(kmsg, kbuf)
    keep(qmsg, qbuf)
    keep(vmsg, vbuf)

    wait_all(kbuf, recv.at[0])
    wait_all(qbuf, recv.at[1])
    wait_all(vbuf, recv.at[2])

    half = pl.ds(pl.multiple_of(core * HD, HD), HD)
    for dt in (2, 1, 3):
        to = (tp + dt) % NT
        send(
            wout.at[half, pl.ds(pl.multiple_of(to * columns, columns), columns)],
            wo.at[NT - dt, half], sent.at[5], recv.at[5], peer_tp(dt),
        )

    nt = (((1,), (1,)), ((), ()))
    blocks = ROWS // QB
    lane_s = lax.broadcasted_iota(jnp.int32, (QB, HD), 1)
    for b in (2, 1, 3, 0):
        rows = pl.ds(b * QB, QB)
        s = lax.dot_general(qbuf[rows, HD:], kbuf[:, :HD], nt, preferred_element_type=F32) * SCALE
        ds = lax.dot_general(qbuf[rows, :], kbuf[...], nt, preferred_element_type=F32) * SCALE
        m = jnp.max(s, axis=1, keepdims=True)
        e = jnp.exp(s - m)
        weighted = e * ds
        l = jnp.sum(e, axis=1, keepdims=True)
        g = jnp.sum(weighted, axis=1, keepdims=True)
        both = jnp.dot(e.astype(BF), vbuf[...], preferred_element_type=F32)
        mix = jnp.dot(weighted.astype(BF), vbuf[:, :HD], preferred_element_type=F32)
        inv = 1.0 / l
        slope = g * inv
        o = both[:, :HD] * inv
        part[rows, :HD] = o.astype(BF)
        part[rows, HD:] = ((both[:, HD:] + mix) * inv - slope * o).astype(BF)
        packed = jnp.where(lane_s == 0, m, jnp.where(lane_s == 1, l, jnp.where(lane_s == 2, slope, 0.0)))
        stat[b] = packed.T[:8, :]
        for dy in (2 * b, 2 * b + 1):
            there = (NY - dy) % NY
            for flip in range(2):
                if dy == 0 and flip == 0:
                    continue
                c = core if flip == 0 else other
                src = pl.ds(pl.multiple_of(dy * 2 * TOK + c * TOK, TOK), TOK)
                send(
                    stat.at[b], sbuf.at[core * NY + there],
                    sent.at[3], recv.at[3], chip_y(dy, c),
                )
                send(
                    part.at[src], pbuf.at[core * NY + there],
                    sent.at[4], recv.at[4], chip_y(dy, c),
                )
    pbuf[core * NY] = part[pl.ds(pl.multiple_of(core * TOK, TOK), TOK), :]
    sbuf[core * NY] = stat[0]

    wait_all(kbuf, sent.at[0])
    wait_all(qbuf, sent.at[1])
    wait_all(vbuf, sent.at[2])

    wait_bytes(sbuf.at[pl.ds(0, peers)], recv.at[3])
    coefs = []
    for head in range(2):
        rows_of = []
        for kind in range(3):
            line = jnp.concatenate([sbuf[head * NY + slot, kind : kind + 1, :] for slot in range(NY)], 0)
            rows_of.append(line)
        odd = lax.broadcasted_iota(jnp.int32, (NY, HD), 0) % 2 == 1
        aligned = []
        for line in rows_of:
            line = jnp.where(odd, pltpu.roll(line, HD // 2, 1), line)
            aligned.append(jnp.where(core == 1, pltpu.roll(line, HD - TOK, 1), line))
        m, l, slope = aligned
        top = jnp.max(m, axis=0, keepdims=True)
        weight = jnp.exp(m - top) * l
        weight = weight / jnp.sum(weight, axis=0, keepdims=True)
        mean_slope = jnp.sum(weight * slope, axis=0, keepdims=True)
        coefs += [weight, weight * (slope - mean_slope)]
    coefs.append(jnp.zeros((HD - 4 * NY, HD), F32))
    table = jnp.concatenate(coefs, 0).T[:TOK, :]
    wait_bytes(pbuf.at[pl.ds(0, peers)], recv.at[4])
    for head in range(2):
        o = jnp.zeros((TOK, HD), F32)
        do = jnp.zeros((TOK, HD), F32)
        for slot in range(NY):
            at = head * 2 * NY + slot
            a = table[:, at : at + 1]
            b = table[:, at + NY : at + NY + 1]
            value = pbuf[head * NY + slot, :, :HD].astype(F32)
            o += a * value
            do += a * pbuf[head * NY + slot, :, HD:].astype(F32) + b * value
        obuf[0, :TOK, head * HD : (head + 1) * HD] = o.astype(BF)
        obuf[0, TOK:, head * HD : (head + 1) * HD] = do.astype(BF)
    for dt in (2, 1, 3):
        send(obuf.at[0], obuf.at[NT - dt], sent.at[6], orecv.at[NT - dt], peer_tp(dt))

    far = pl.ds(1, NT - 1)
    wait_bytes(wo.at[far, half], recv.at[5])
    send(wo.at[far, half], wo.at[far, half], sent.at[7], recv.at[6], sibling)
    wait_bytes(sbuf.at[pl.ds(0, peers)], sent.at[3])
    wait_bytes(pbuf.at[pl.ds(0, peers)], sent.at[4])
    get_wo.wait()
    total = jnp.dot(obuf[0], wo[0], preferred_element_type=F32)
    wait_bytes(wo.at[far, half], recv.at[6])
    for dt in (1, 3, 2):
        wait_bytes(obuf.at[0], orecv.at[dt])
        total += jnp.dot(obuf[dt], wo[dt], preferred_element_type=F32)
    out[...] = total.astype(BF)
    wait_bytes(wo.at[far, half], sent.at[5])
    wait_bytes(wo.at[far, half], sent.at[7])
    wait_bytes(obuf.at[far], sent.at[6])


def on_device(hidden_in, hidden_tan, qkv_weight, out_weight, norm_gain, pos_local, tile_anchor):
    quarter = HD // 4
    frequency = np.float32(THETA) ** (-np.arange(quarter, dtype=np.float32) / np.float32(quarter))
    freq = jnp.asarray(np.tile(frequency.astype(np.float32), (8, 4)))
    hbm = pl.BlockSpec(memory_space=pltpu.HBM)
    vmem = pl.BlockSpec(memory_space=pltpu.VMEM)
    dma = pltpu.SemaphoreType.DMA
    columns = NT * HD
    operands = (
        hidden_in, hidden_tan, qkv_weight, out_weight, norm_gain, pos_local,
        tile_anchor.reshape(1, 2), freq,
    )
    both = pl.pallas_call(
        kernel,
        out_shape=pltpu.VMEM((2 * TOK, columns), BF),
        in_specs=[hbm] * 8,
        out_specs=vmem,
        scratch_shapes=[
            pltpu.VMEM((2 * TOK, 2048), BF),
            pltpu.VMEM((3, 2048, 2 * HD), BF),
            pltpu.VMEM((NT, 2 * HD, columns), BF),
            pltpu.VMEM((2, HD), F32),
            pltpu.VMEM((2, TOK), jnp.int32),
            pltpu.VMEM((1, 2), jnp.int32),
            pltpu.VMEM((8, HD), F32),
            pltpu.VMEM((2, TOK, 2 * HD), BF),
            pltpu.VMEM((2, TOK, 2 * HD), BF),
            pltpu.VMEM((2, TOK, 2 * HD), BF),
            pltpu.VMEM((ROWS, 2 * HD), BF),
            pltpu.VMEM((ROWS, 2 * HD), BF),
            pltpu.VMEM((ROWS, 2 * HD), BF),
            pltpu.VMEM((ROWS, 2 * HD), BF),
            pltpu.VMEM((ROWS // QB, 8, HD), F32),
            pltpu.VMEM((2 * NY, TOK, 2 * HD), BF),
            pltpu.VMEM((2 * NY, 8, HD), F32),
            pltpu.VMEM((NT, 2 * TOK, 2 * HD), BF),
            dma((10,)),
            dma((8,)),
            dma((7,)),
            dma((NT,)),
        ],
        compiler_params=pltpu.CompilerParams(
            collective_id=0, has_side_effects=True, vmem_limit_bytes=40 * 2**20
        ),
    )(*[pltpu.with_memory_space_constraint(a, pltpu.HBM) for a in operands])
    return both[:TOK], both[TOK:]


def solution(mesh):
    in_specs = (
        P("ctx", None),
        P("ctx", None),
        P(None, None, "tp"),
        P("tp", None),
        P(),
        P(None, "ctx"),
        P(None, "ctx"),
    )
    out_specs = (P("ctx", "tp"), P("ctx", "tp"))
    return jax.shard_map(
        on_device, mesh=mesh, in_specs=in_specs, out_specs=out_specs, check_vma=False
    )
```

```python
import numpy as np
import jax
import jax.numpy as jnp
from jax import lax
from jax.experimental import pallas as pl
from jax.experimental.pallas import tpu as pltpu
from jax.sharding import PartitionSpec as P

THETA = 10000.0
MESH = pl.DeviceIdType.MESH
BF = jnp.bfloat16
F32 = jnp.float32

TOK = 32
HALF = TOK // 2
HD = 128
NX, NY, NZ, NT = 4, 8, 2, 4
ROWS = NY * 2 * TOK
QB = 128
SCALE = HD**-0.5

XZ = [(2, 1), (1, 1), (3, 1), (2, 0), (1, 0), (3, 0), (0, 1), (0, 0)]
YS = [4, 3, 5, 2, 6, 1, 7, 0]


def slot_xz(dx, dz):
    return (dx % NX) * NZ + dz % NZ


def sin_cos(x):
    k = jnp.floor(x * 0.6366197723675814 + 0.5)
    r = ((x - k * 1.5703125) - k * 4.837512969970703125e-4) - k * 7.54978995489188216e-8
    r2 = r * r
    s = r + r * r2 * (-1.6666654611e-1 + r2 * (8.3321608736e-3 + r2 * -1.9515295891e-4))
    c = 1.0 - 0.5 * r2 + r2 * r2 * (
        4.166664568298827e-2 + r2 * (-1.388731625493765e-3 + r2 * 2.443315711809948e-5)
    )
    quad = k - 4.0 * jnp.floor(k * 0.25)
    odd = (quad == 1.0) | (quad == 3.0)
    sin = jnp.where(odd, c, s)
    cos = jnp.where(odd, s, c)
    sin = jnp.where(quad >= 2.0, -sin, sin)
    cos = jnp.where((quad == 1.0) | (quad == 2.0), -cos, cos)
    return sin, cos


def kernel(
    hin, htan, wqkv, wout, gain, pos, anchor, freq,
    out,
    h, w, wo, gain_v, pos_v, anchor_v, freq_v,
    kmsg, qmsg, vmsg, kbuf, qbuf, vbuf, part, stat, pbuf, sbuf, obuf,
    loc, sent, recv, orecv,
):
    ctx = lax.axis_index("ctx")
    tp = lax.axis_index("tp")
    z, x, y, core = ctx // 64, (ctx // 16) % NX, (ctx // 2) % NY, ctx % 2

    def chip_xz(dx, dz, c):
        return {"ctx": ((((z + dz) % NZ) * NX + (x + dx) % NX) * NY + y) * 2 + c}

    def chip_y(dy, c):
        return {"ctx": ((z * NX + x) * NY + (y + dy) % NY) * 2 + c}

    def peer_tp(dt):
        return {"tp": (tp + dt) % NT}

    other = 1 - core
    sibling = {"ctx": ctx + 1 - 2 * core}

    barrier = pltpu.get_barrier_semaphore()
    count = 0
    for c in range(2):
        for dy in YS[:-1]:
            pl.semaphore_signal(barrier, inc=1, device_id=chip_y(dy, c), device_id_type=MESH)
            count += 1
        for dx, dz in XZ[:-1]:
            pl.semaphore_signal(barrier, inc=1, device_id=chip_xz(dx, dz, c), device_id_type=MESH)
            count += 1
    for dt in (1, 2, 3):
        pl.semaphore_signal(barrier, inc=1, device_id=peer_tp(dt), device_id_type=MESH)
        count += 1
    pl.semaphore_signal(barrier, inc=1, device_id=sibling, device_id_type=MESH)
    count += 1

    def fetch(i, src, dst):
        copy = pltpu.make_async_copy(src, dst, loc.at[i])
        copy.start()
        return copy

    get_pos = fetch(0, pos, pos_v)
    get_anchor = fetch(1, anchor, anchor_v)
    get_freq = fetch(2, freq, freq_v)
    get_hin = fetch(3, hin, h.at[pl.ds(0, TOK)])
    get_htan = fetch(4, htan, h.at[pl.ds(TOK, TOK)])
    get_wk = fetch(5, wqkv.at[1], w.at[1])
    get_gain = fetch(6, gain, gain_v)
    get_wq = fetch(7, wqkv.at[0], w.at[0])
    get_wv = fetch(8, wqkv.at[2], w.at[2])
    columns = NT * HD
    get_wo = fetch(9, wout.at[:, pl.ds(pl.multiple_of(tp * columns, columns), columns)], wo.at[0])

    get_pos.wait()
    get_anchor.wait()
    get_freq.wait()
    row_place = pos_v[0:1, :] + anchor_v[:, 0:1]
    col_place = pos_v[1:2, :] + anchor_v[:, 1:2]
    eye = lax.broadcasted_iota(jnp.int32, (TOK, TOK), 0) == lax.broadcasted_iota(
        jnp.int32, (TOK, TOK), 1
    )
    row_id = jnp.sum(jnp.where(eye, row_place.astype(F32), 0.0), axis=1, keepdims=True)
    col_id = jnp.sum(jnp.where(eye, col_place.astype(F32), 0.0), axis=1, keepdims=True)
    lane = lax.broadcasted_iota(jnp.int32, (TOK, HD), 1)
    sine, cosine = sin_cos(jnp.where(lane < HD // 2, row_id, col_id) * freq_v[0:1, :])
    low = lane % (HD // 2) < HD // 4
    sine = jnp.where(low, -sine, sine)

    def rotate(n):
        wide = n.astype(BF).astype(F32)
        turned = jnp.where(low, pltpu.roll(wide, HD - HD // 4, 1), pltpu.roll(wide, HD // 4, 1))
        return (wide * cosine + turned * sine).astype(BF)

    def norm_rotate(projected, row, head):
        g = gain_v[row : row + 1, :]
        raw = projected[:TOK, head * HD : (head + 1) * HD]
        tan = projected[TOK:, head * HD : (head + 1) * HD]
        ms = jnp.mean(raw * raw, axis=1, keepdims=True) + 1e-06
        r = lax.rsqrt(ms)
        cross = jnp.mean(raw * tan, axis=1, keepdims=True)
        n = raw * r * g
        dn = g * r * (tan - raw * (cross / ms))
        return rotate(n), rotate(dn)

    def project(which):
        return jnp.dot(h[...], w[which], preferred_element_type=F32)

    def own_rows(slot):
        return pl.ds(pl.multiple_of(slot * 2 * TOK + core * TOK, TOK), TOK)

    def send(src, dst, ssem, rsem, device):
        copy = pltpu.make_async_remote_copy(
            src_ref=src, dst_ref=dst, send_sem=ssem, recv_sem=rsem,
            device_id=device, device_id_type=MESH,
        )
        copy.start()

    def spread_xz(msg, buf, ssem, rsem):
        for dx, dz in XZ:
            there = slot_xz(-dx, -dz)
            for flip in range(2):
                if (dx, dz) == (0, 0) and flip == 0:
                    continue
                c = core if flip == 0 else other
                send(
                    msg.at[c], buf.at[own_rows(there)],
                    ssem, rsem, chip_xz(dx, dz, c),
                )

    def spread_y(msg, buf, ssem, rsem):
        for dy in YS:
            there = (NY - dy) % NY
            for flip in range(2):
                if dy == 0 and flip == 0:
                    continue
                c = core if flip == 0 else other
                send(
                    msg.at[c], buf.at[own_rows(there)],
                    ssem, rsem, chip_y(dy, c),
                )

    def keep(msg, buf):
        buf[own_rows(0), :] = msg[core]

    def wait_bytes(ref, sem):
        pltpu.make_async_copy(ref, ref, sem).wait()

    peers = 2 * NY - 1

    def wait_all(buf, sem):
        wait_bytes(buf.at[pl.ds(0, peers * TOK)], sem)

    get_gain.wait()
    get_hin.wait()
    get_htan.wait()
    get_wk.wait()
    projected = project(1)
    for head in range(2):
        k, dk = norm_rotate(projected, 1, head)
        kmsg[head, :, :HD] = k
        kmsg[head, :, HD:] = dk
    pl.semaphore_wait(barrier, count)
    spread_xz(kmsg, kbuf, sent.at[0], recv.at[0])
    get_wq.wait()
    projected = project(0)
    for head in range(2):
        q, dq = norm_rotate(projected, 0, head)
        qmsg[head, :, :HD] = dq
        qmsg[head, :, HD:] = q
    spread_y(qmsg, qbuf, sent.at[1], recv.at[1])
    get_wv.wait()
    projected = project(2)
    for head in range(2):
        vmsg[head, :, :HD] = projected[:TOK, head * HD : (head + 1) * HD].astype(BF)
        vmsg[head, :, HD:] = projected[TOK:, head * HD : (head + 1) * HD].astype(BF)
    spread_xz(vmsg, vbuf, sent.at[2], recv.at[2])
    keep(kmsg, kbuf)
    keep(qmsg, qbuf)
    keep(vmsg, vbuf)

    wait_all(kbuf, recv.at[0])
    wait_all(qbuf, recv.at[1])
    wait_all(vbuf, recv.at[2])

    half = pl.ds(pl.multiple_of(core * HD, HD), HD)
    quarter = pl.ds(pl.multiple_of(core * HD + x * TOK, TOK), TOK)
    far = pl.ds(1, NT - 1)
    for dt in (2, 1, 3):
        to = (tp + dt) % NT
        send(
            wout.at[quarter, pl.ds(pl.multiple_of(to * columns, columns), columns)],
            wo.at[NT - dt, quarter], sent.at[5], recv.at[5], peer_tp(dt),
        )

    nt = (((1,), (1,)), ((), ()))
    blocks = ROWS // QB
    lane_s = lax.broadcasted_iota(jnp.int32, (QB, HD), 1)
    for b in (2, 1, 3, 0):
        rows = pl.ds(b * QB, QB)
        s = lax.dot_general(qbuf[rows, HD:], kbuf[:, :HD], nt, preferred_element_type=F32) * SCALE
        ds = lax.dot_general(qbuf[rows, :], kbuf[...], nt, preferred_element_type=F32) * SCALE
        m = jnp.max(s, axis=1, keepdims=True)
        e = jnp.exp(s - m)
        weighted = e * ds
        l = jnp.sum(e, axis=1, keepdims=True)
        g = jnp.sum(weighted, axis=1, keepdims=True)
        both = jnp.dot(e.astype(BF), vbuf[...], preferred_element_type=F32)
        mix = jnp.dot(weighted.astype(BF), vbuf[:, :HD], preferred_element_type=F32)
        inv = 1.0 / l
        slope = g * inv
        o = both[:, :HD] * inv
        part[rows, :HD] = o.astype(BF)
        part[rows, HD:] = ((both[:, HD:] + mix) * inv - slope * o).astype(BF)
        packed = jnp.where(lane_s == 0, m, jnp.where(lane_s == 1, l, jnp.where(lane_s == 2, slope, 0.0)))
        stat[b] = packed.T[:8, :]
        for dy in (2 * b, 2 * b + 1):
            there = (NY - dy) % NY
            for flip in range(2):
                if dy == 0 and flip == 0:
                    continue
                c = core if flip == 0 else other
                src = pl.ds(pl.multiple_of(dy * 2 * TOK + c * TOK, HALF), HALF)
                send(
                    stat.at[b], sbuf.at[core * NY + there],
                    sent.at[3], recv.at[3], chip_y(dy, c),
                )
                send(
                    part.at[src], pbuf.at[0, core * NY + there],
                    sent.at[4], recv.at[4], chip_y(dy, c),
                )
    for dy in (4, 5, 2, 3, 6, 7, 1, 0):
        there = (NY - dy) % NY
        for flip in range(2):
            if dy == 0 and flip == 0:
                continue
            c = core if flip == 0 else other
            src = pl.ds(pl.multiple_of(dy * 2 * TOK + c * TOK + HALF, HALF), HALF)
            send(
                part.at[src], pbuf.at[1, core * NY + there],
                sent.at[9], recv.at[8], chip_y(dy, c),
            )
    for piece in range(2):
        own = pl.ds(pl.multiple_of(core * TOK + piece * HALF, HALF), HALF)
        pbuf[piece, core * NY] = part[own, :]
    sbuf[core * NY] = stat[0]

    wait_bytes(wo.at[far, quarter], recv.at[5])
    for dx in (2, 1, 3):
        send(wo.at[far, quarter], wo.at[far, quarter], sent.at[7], recv.at[7], chip_xz(dx, 0, core))

    wait_all(kbuf, sent.at[0])
    wait_all(qbuf, sent.at[1])
    wait_all(vbuf, sent.at[2])

    wait_bytes(sbuf.at[pl.ds(0, peers)], recv.at[3])
    coefs = []
    for head in range(2):
        rows_of = []
        for kind in range(3):
            line = jnp.concatenate([sbuf[head * NY + slot, kind : kind + 1, :] for slot in range(NY)], 0)
            rows_of.append(line)
        odd = lax.broadcasted_iota(jnp.int32, (NY, HD), 0) % 2 == 1
        aligned = []
        for line in rows_of:
            line = jnp.where(odd, pltpu.roll(line, HD // 2, 1), line)
            aligned.append(jnp.where(core == 1, pltpu.roll(line, HD - TOK, 1), line))
        m, l, slope = aligned
        top = jnp.max(m, axis=0, keepdims=True)
        weight = jnp.exp(m - top) * l
        weight = weight / jnp.sum(weight, axis=0, keepdims=True)
        mean_slope = jnp.sum(weight * slope, axis=0, keepdims=True)
        coefs += [weight, weight * (slope - mean_slope)]
    coefs.append(jnp.zeros((HD - 4 * NY, HD), F32))
    table = jnp.concatenate(coefs, 0).T[:TOK, :]
    for piece in range(2):
        wait_bytes(pbuf.at[0, pl.ds(0, peers)], recv.at[4 if piece == 0 else 8])
        for head in range(2):
            o = jnp.zeros((HALF, HD), F32)
            do = jnp.zeros((HALF, HD), F32)
            for slot in range(NY):
                at = head * 2 * NY + slot
                a = table[piece * HALF : (piece + 1) * HALF, at : at + 1]
                b = table[piece * HALF : (piece + 1) * HALF, at + NY : at + NY + 1]
                value = pbuf[piece, head * NY + slot, :, :HD].astype(F32)
                o += a * value
                do += a * pbuf[piece, head * NY + slot, :, HD:].astype(F32) + b * value
            obuf[0, piece * TOK : piece * TOK + HALF, head * HD : (head + 1) * HD] = o.astype(BF)
            obuf[0, piece * TOK + HALF : (piece + 1) * TOK, head * HD : (head + 1) * HD] = do.astype(BF)
        rows = pl.ds(piece * TOK, TOK)
        for dt in (2, 1, 3):
            send(
                obuf.at[0, rows], obuf.at[NT - dt, rows],
                sent.at[6], orecv.at[NT - dt], peer_tp(dt),
            )

    wait_bytes(wo.at[far, pl.ds(0, 3 * TOK)], recv.at[7])
    send(wo.at[far, half], wo.at[far, half], sent.at[8], recv.at[6], sibling)
    wait_bytes(sbuf.at[pl.ds(0, peers)], sent.at[3])
    wait_bytes(pbuf.at[0, pl.ds(0, peers)], sent.at[4])
    wait_bytes(pbuf.at[0, pl.ds(0, peers)], sent.at[9])
    get_wo.wait()
    total = jnp.dot(obuf[0], wo[0], preferred_element_type=F32)
    wait_bytes(wo.at[far, half], recv.at[6])
    for dt in (1, 3, 2):
        wait_bytes(obuf.at[0], orecv.at[dt])
        total += jnp.dot(obuf[dt], wo[dt], preferred_element_type=F32)
    rounded = total.astype(BF)
    for piece in range(2):
        for kind in range(2):
            at = piece * TOK + kind * HALF
            out[kind * TOK + piece * HALF : kind * TOK + (piece + 1) * HALF, :] = rounded[at : at + HALF, :]
    wait_bytes(wo.at[far, quarter], sent.at[5])
    wait_bytes(wo.at[far, pl.ds(0, 3 * TOK)], sent.at[7])
    wait_bytes(wo.at[far, half], sent.at[8])
    wait_bytes(obuf.at[far], sent.at[6])


def on_device(hidden_in, hidden_tan, qkv_weight, out_weight, norm_gain, pos_local, tile_anchor):
    quarter = HD // 4
    frequency = np.float32(THETA) ** (-np.arange(quarter, dtype=np.float32) / np.float32(quarter))
    freq = jnp.asarray(np.tile(frequency.astype(np.float32), (8, 4)))
    hbm = pl.BlockSpec(memory_space=pltpu.HBM)
    vmem = pl.BlockSpec(memory_space=pltpu.VMEM)
    dma = pltpu.SemaphoreType.DMA
    columns = NT * HD
    operands = (
        hidden_in, hidden_tan, qkv_weight, out_weight, norm_gain, pos_local,
        tile_anchor.reshape(1, 2), freq,
    )
    both = pl.pallas_call(
        kernel,
        out_shape=pltpu.VMEM((2 * TOK, columns), BF),
        in_specs=[hbm] * 8,
        out_specs=vmem,
        scratch_shapes=[
            pltpu.VMEM((2 * TOK, 2048), BF),
            pltpu.VMEM((3, 2048, 2 * HD), BF),
            pltpu.VMEM((NT, 2 * HD, columns), BF),
            pltpu.VMEM((2, HD), F32),
            pltpu.VMEM((2, TOK), jnp.int32),
            pltpu.VMEM((1, 2), jnp.int32),
            pltpu.VMEM((8, HD), F32),
            pltpu.VMEM((2, TOK, 2 * HD), BF),
            pltpu.VMEM((2, TOK, 2 * HD), BF),
            pltpu.VMEM((2, TOK, 2 * HD), BF),
            pltpu.VMEM((ROWS, 2 * HD), BF),
            pltpu.VMEM((ROWS, 2 * HD), BF),
            pltpu.VMEM((ROWS, 2 * HD), BF),
            pltpu.VMEM((ROWS, 2 * HD), BF),
            pltpu.VMEM((ROWS // QB, 8, HD), F32),
            pltpu.VMEM((2, 2 * NY, HALF, 2 * HD), BF),
            pltpu.VMEM((2 * NY, 8, HD), F32),
            pltpu.VMEM((NT, 2 * TOK, 2 * HD), BF),
            dma((10,)),
            dma((10,)),
            dma((9,)),
            dma((NT,)),
        ],
        compiler_params=pltpu.CompilerParams(
            collective_id=0, has_side_effects=True, vmem_limit_bytes=40 * 2**20
        ),
    )(*[pltpu.with_memory_space_constraint(a, pltpu.HBM) for a in operands])
    return both[:TOK], both[TOK:]


def solution(mesh):
    in_specs = (
        P("ctx", None),
        P("ctx", None),
        P(None, None, "tp"),
        P("tp", None),
        P(),
        P(None, "ctx"),
        P(None, "ctx"),
    )
    out_specs = (P("ctx", "tp"), P("ctx", "tp"))
    return jax.shard_map(
        on_device, mesh=mesh, in_specs=in_specs, out_specs=out_specs, check_vma=False
    )
```

```python
import functools

import numpy as np
import jax
import jax.numpy as jnp
from jax import lax
from jax.experimental import pallas as pl
from jax.experimental.pallas import tpu as pltpu
from jax.sharding import PartitionSpec as P

THETA = 10000.0
MESH = pl.DeviceIdType.MESH
BF = jnp.bfloat16
F32 = jnp.float32

TOK = 32
HALF = TOK // 2
HD = 128
NX, NY, NZ, NT = 4, 8, 2, 4
ROWS = NY * 2 * TOK
QB = 128
SCALE = HD**-0.5

XZ = [(2, 1), (1, 1), (3, 1), (2, 0), (1, 0), (3, 0), (0, 1), (0, 0)]
YS = [4, 3, 5, 2, 6, 1, 7, 0]


def slot_xz(dx, dz):
    return (dx % NX) * NZ + dz % NZ


def sin_cos(x):
    k = jnp.floor(x * 0.6366197723675814 + 0.5)
    r = ((x - k * 1.5703125) - k * 4.837512969970703125e-4) - k * 7.54978995489188216e-8
    r2 = r * r
    s = r + r * r2 * (-1.6666654611e-1 + r2 * (8.3321608736e-3 + r2 * -1.9515295891e-4))
    c = 1.0 - 0.5 * r2 + r2 * r2 * (
        4.166664568298827e-2 + r2 * (-1.388731625493765e-3 + r2 * 2.443315711809948e-5)
    )
    quad = k - 4.0 * jnp.floor(k * 0.25)
    odd = (quad == 1.0) | (quad == 3.0)
    sin = jnp.where(odd, c, s)
    cos = jnp.where(odd, s, c)
    sin = jnp.where(quad >= 2.0, -sin, sin)
    cos = jnp.where((quad == 1.0) | (quad == 2.0), -cos, cos)
    return sin, cos


def split(value):
    near = value.astype(BF)
    return near, (value - near.astype(F32)).astype(BF)


def kernel(
    hin, htan, wqkv, wout, gain, pos, anchor, freq,
    out,
    h, w, wo, gain_v, pos_v, anchor_v, freq_v,
    kmsg, qmsg, vmsg, kbuf, qbuf, vbuf, part, stat, pbuf, sbuf, obuf,
    loc, sent, recv, orecv, ready,
):
    ctx = lax.axis_index("ctx")
    tp = lax.axis_index("tp")
    z, x, y, core = ctx // 64, (ctx // 16) % NX, (ctx // 2) % NY, ctx % 2

    def chip_xz(dx, dz, c):
        return {"ctx": ((((z + dz) % NZ) * NX + (x + dx) % NX) * NY + y) * 2 + c}

    def chip_y(dy, c):
        return {"ctx": ((z * NX + x) * NY + (y + dy) % NY) * 2 + c}

    def peer_tp(dt):
        return {"tp": (tp + dt + NT) % NT}

    other = 1 - core
    sibling = {"ctx": ctx + 1 - 2 * core}

    barrier = pltpu.get_barrier_semaphore()
    count = 0
    for c in range(2):
        for dy in YS[:-1]:
            pl.semaphore_signal(barrier, inc=1, device_id=chip_y(dy, c), device_id_type=MESH)
            count += 1
        for dx, dz in XZ[:-1]:
            pl.semaphore_signal(barrier, inc=1, device_id=chip_xz(dx, dz, c), device_id_type=MESH)
            count += 1
    pl.semaphore_signal(barrier, inc=1, device_id=sibling, device_id_type=MESH)
    count += 1
    for k in (1, 2, 3):

        @pl.when(tp + k < NT)
        def _():
            pl.semaphore_signal(barrier, inc=1, device_id=peer_tp(k), device_id_type=MESH)


    def fetch(i, src, dst):
        copy = pltpu.make_async_copy(src, dst, loc.at[i])
        copy.start()
        return copy

    get_pos = fetch(0, pos, pos_v)
    get_anchor = fetch(1, anchor, anchor_v)
    get_freq = fetch(2, freq, freq_v)
    get_hin = fetch(3, hin, h.at[pl.ds(0, TOK)])
    get_htan = fetch(4, htan, h.at[pl.ds(TOK, TOK)])
    get_wk = fetch(5, wqkv.at[1], w.at[1])
    get_gain = fetch(6, gain, gain_v)
    get_wq = fetch(7, wqkv.at[0], w.at[0])
    get_wv = fetch(8, wqkv.at[2], w.at[2])
    columns = NT * HD
    get_wo = fetch(9, wout.at[:, pl.ds(pl.multiple_of(tp * columns, columns), columns)], wo.at[0])

    get_pos.wait()
    get_anchor.wait()
    get_freq.wait()
    row_place = pos_v[0:1, :] + anchor_v[:, 0:1]
    col_place = pos_v[1:2, :] + anchor_v[:, 1:2]
    eye = lax.broadcasted_iota(jnp.int32, (TOK, TOK), 0) == lax.broadcasted_iota(
        jnp.int32, (TOK, TOK), 1
    )
    row_id = jnp.sum(jnp.where(eye, row_place.astype(F32), 0.0), axis=1, keepdims=True)
    col_id = jnp.sum(jnp.where(eye, col_place.astype(F32), 0.0), axis=1, keepdims=True)
    lane = lax.broadcasted_iota(jnp.int32, (TOK, HD), 1)
    sine, cosine = sin_cos(jnp.where(lane < HD // 2, row_id, col_id) * freq_v[0:1, :])
    low = lane % (HD // 2) < HD // 4
    sine = jnp.where(low, -sine, sine)

    def rotate(n):
        wide = n.astype(BF).astype(F32)
        turned = jnp.where(low, pltpu.roll(wide, HD - HD // 4, 1), pltpu.roll(wide, HD // 4, 1))
        return (wide * cosine + turned * sine).astype(BF)

    def norm_rotate(projected, row, head):
        g = gain_v[row : row + 1, :]
        raw = projected[:TOK, head * HD : (head + 1) * HD]
        tan = projected[TOK:, head * HD : (head + 1) * HD]
        ms = jnp.mean(raw * raw, axis=1, keepdims=True) + 1e-06
        r = lax.rsqrt(ms)
        cross = jnp.mean(raw * tan, axis=1, keepdims=True)
        n = raw * r * g
        dn = g * r * (tan - raw * (cross / ms))
        return rotate(n), rotate(dn)

    def project(which):
        return jnp.dot(h[...], w[which], preferred_element_type=F32)

    def own_rows(slot):
        return pl.ds(pl.multiple_of(slot * 2 * TOK + core * TOK, TOK), TOK)

    def send(src, dst, ssem, rsem, device):
        copy = pltpu.make_async_remote_copy(
            src_ref=src, dst_ref=dst, send_sem=ssem, recv_sem=rsem,
            device_id=device, device_id_type=MESH,
        )
        copy.start()

    def spread_xz(msg, buf, ssem, rsem):
        for dx, dz in XZ:
            there = slot_xz(-dx, -dz)
            for flip in range(2):
                if (dx, dz) == (0, 0) and flip == 0:
                    continue
                c = core if flip == 0 else other
                send(
                    msg.at[c], buf.at[own_rows(there)],
                    ssem, rsem, chip_xz(dx, dz, c),
                )

    def spread_y(msg, buf, ssem, rsem):
        for dy in YS:
            there = (NY - dy) % NY
            for flip in range(2):
                if dy == 0 and flip == 0:
                    continue
                c = core if flip == 0 else other
                send(
                    msg.at[c], buf.at[own_rows(there)],
                    ssem, rsem, chip_y(dy, c),
                )

    def keep(msg, buf):
        buf[own_rows(0), :] = msg[core]

    def wait_bytes(ref, sem):
        pltpu.make_async_copy(ref, ref, sem).wait()

    peers = 2 * NY - 1

    def wait_all(buf, sem):
        wait_bytes(buf.at[pl.ds(0, peers * TOK)], sem)

    get_gain.wait()
    get_hin.wait()
    get_htan.wait()
    get_wk.wait()
    projected = project(1)
    for head in range(2):
        k, dk = norm_rotate(projected, 1, head)
        kmsg[head, :, :HD] = k
        kmsg[head, :, HD:] = dk
    pl.semaphore_wait(barrier, count + tp)
    for k in (3, 2, 1):

        @pl.when(tp >= k)
        def _():
            pl.semaphore_signal(ready.at[k], inc=1, device_id=peer_tp(-k), device_id_type=MESH)

    spread_xz(kmsg, kbuf, sent.at[0], recv.at[0])
    get_wq.wait()
    projected = project(0)
    for head in range(2):
        q, dq = norm_rotate(projected, 0, head)
        qmsg[head, :, :HD] = dq
        qmsg[head, :, HD:] = q
    spread_y(qmsg, qbuf, sent.at[1], recv.at[1])
    get_wv.wait()
    projected = project(2)
    for head in range(2):
        vmsg[head, :, :HD] = projected[:TOK, head * HD : (head + 1) * HD].astype(BF)
        vmsg[head, :, HD:] = projected[TOK:, head * HD : (head + 1) * HD].astype(BF)
    spread_xz(vmsg, vbuf, sent.at[2], recv.at[2])
    keep(kmsg, kbuf)
    keep(qmsg, qbuf)
    keep(vmsg, vbuf)

    wait_all(kbuf, recv.at[0])
    wait_all(qbuf, recv.at[1])
    wait_all(vbuf, recv.at[2])

    half = pl.ds(pl.multiple_of(core * HD, HD), HD)
    quarter = pl.ds(pl.multiple_of(core * HD + x * TOK, TOK), TOK)
    far = pl.ds(1, NT - 1)

    def send_columns(dt):
        to = (tp + dt + NT) % NT
        send(
            wout.at[quarter, pl.ds(pl.multiple_of(to * columns, columns), columns)],
            wo.at[(NT - dt) % NT, quarter], sent.at[5], recv.at[5], peer_tp(dt),
        )

    for k in (3, 2, 1):
        pl.when(tp >= k)(functools.partial(send_columns, -k))

    nt = (((1,), (1,)), ((), ()))
    blocks = ROWS // QB
    lane_s = lax.broadcasted_iota(jnp.int32, (QB, HD), 1)
    for b in (2, 1, 3, 0):
        rows = pl.ds(b * QB, QB)
        s = lax.dot_general(qbuf[rows, HD:], kbuf[:, :HD], nt, preferred_element_type=F32) * SCALE
        ds = lax.dot_general(qbuf[rows, :], kbuf[...], nt, preferred_element_type=F32) * SCALE
        m = jnp.max(s, axis=1, keepdims=True)
        e = jnp.exp(s - m)
        weighted = e * ds
        l = jnp.sum(e, axis=1, keepdims=True)
        g = jnp.sum(weighted, axis=1, keepdims=True)
        e, e_rest = split(e)
        weighted, weighted_rest = split(weighted)
        both = jnp.dot(e, vbuf[...], preferred_element_type=F32)
        both += jnp.dot(e_rest, vbuf[...], preferred_element_type=F32)
        mix = jnp.dot(weighted, vbuf[:, :HD], preferred_element_type=F32)
        mix += jnp.dot(weighted_rest, vbuf[:, :HD], preferred_element_type=F32)
        inv = 1.0 / l
        slope = g * inv
        o = both[:, :HD] * inv
        part[rows, :HD] = o.astype(BF)
        part[rows, HD:] = ((both[:, HD:] + mix) * inv - slope * o).astype(BF)
        packed = jnp.where(lane_s == 0, m, jnp.where(lane_s == 1, l, jnp.where(lane_s == 2, slope, 0.0)))
        lines = packed.T[:8, :]
        turns = [lines] + [pltpu.roll(lines, HD - TOK * k, 1) for k in range(1, 4)]
        for j in range(4):
            stat[4 * b + j] = jnp.where(
                lane_s[:1] < TOK,
                turns[j][0:1],
                jnp.where(lane_s[:1] < 2 * TOK, turns[(j + 3) % 4][1:2], turns[(j + 2) % 4][2:3]),
            )
        for dy in (2 * b, 2 * b + 1):
            there = (NY - dy) % NY
            for flip in range(2):
                if dy == 0 and flip == 0:
                    continue
                c = core if flip == 0 else other
                src = pl.ds(pl.multiple_of(dy * 2 * TOK + c * TOK, HALF), HALF)
                send(
                    stat.at[2 * dy + c], sbuf.at[core * NY + there],
                    sent.at[3], recv.at[3], chip_y(dy, c),
                )
                send(
                    part.at[src], pbuf.at[0, core * NY + there],
                    sent.at[4], recv.at[4], chip_y(dy, c),
                )
    for dy in (4, 5, 2, 3, 6, 7, 1, 0):
        there = (NY - dy) % NY
        for flip in range(2):
            if dy == 0 and flip == 0:
                continue
            c = core if flip == 0 else other
            src = pl.ds(pl.multiple_of(dy * 2 * TOK + c * TOK + HALF, HALF), HALF)
            send(
                part.at[src], pbuf.at[1, core * NY + there],
                sent.at[9], recv.at[8], chip_y(dy, c),
            )
    for piece in range(2):
        own = pl.ds(pl.multiple_of(core * TOK + piece * HALF, HALF), HALF)
        pbuf[piece, core * NY] = part[own, :]
    sbuf[core * NY] = stat[core]

    for k in (1, 2, 3):

        @pl.when(tp + k < NT)
        def _():
            pl.semaphore_wait(ready.at[k], 1)
            send_columns(k)

    wait_bytes(wo.at[far, quarter], recv.at[5])
    for dx in (2, 1, 3):
        send(wo.at[far, quarter], wo.at[far, quarter], sent.at[7], recv.at[7], chip_xz(dx, 0, core))

    wait_all(kbuf, sent.at[0])
    wait_all(qbuf, sent.at[1])
    wait_all(vbuf, sent.at[2])

    wait_bytes(sbuf.at[pl.ds(0, peers)], recv.at[3])
    coefs = []
    for head in range(2):
        m = jnp.concatenate([sbuf[head * NY + slot] for slot in range(NY)], 0)
        l = pltpu.roll(m, HD - TOK, 1)
        slope = pltpu.roll(m, HD - 2 * TOK, 1)
        top = jnp.max(m, axis=0, keepdims=True)
        weight = jnp.exp(m - top) * l
        weight = weight / jnp.sum(weight, axis=0, keepdims=True)
        mean_slope = jnp.sum(weight * slope, axis=0, keepdims=True)
        coefs += [weight, weight * (slope - mean_slope)]
    coefs.append(jnp.zeros((HD - 4 * NY, HD), F32))
    table = jnp.concatenate(coefs, 0).T[:TOK, :]
    for piece in range(2):
        wait_bytes(pbuf.at[0, pl.ds(0, peers)], recv.at[4 if piece == 0 else 8])
        for head in range(2):
            o = jnp.zeros((HALF, HD), F32)
            do = jnp.zeros((HALF, HD), F32)
            for slot in range(NY):
                at = head * 2 * NY + slot
                a = table[piece * HALF : (piece + 1) * HALF, at : at + 1]
                b = table[piece * HALF : (piece + 1) * HALF, at + NY : at + NY + 1]
                value = pbuf[piece, head * NY + slot, :, :HD].astype(F32)
                o += a * value
                do += a * pbuf[piece, head * NY + slot, :, HD:].astype(F32) + b * value
            obuf[0, piece * TOK : piece * TOK + HALF, head * HD : (head + 1) * HD] = o.astype(BF)
            obuf[0, piece * TOK + HALF : (piece + 1) * TOK, head * HD : (head + 1) * HD] = do.astype(BF)
        rows = pl.ds(piece * TOK, TOK)

        def send_rows(dt, rows):
            send(
                obuf.at[0, rows], obuf.at[(NT - dt) % NT, rows],
                sent.at[6], orecv.at[(NT - dt) % NT], peer_tp(dt),
            )

        for k in (3, 2, 1):
            pl.when(tp >= k)(functools.partial(send_rows, -k, rows))
    for k in (1, 2, 3):

        @pl.when(tp + k < NT)
        def _():
            send_rows(k, pl.ds(0, 2 * TOK))


    wait_bytes(wo.at[far, pl.ds(0, 3 * TOK)], recv.at[7])
    send(wo.at[far, half], wo.at[far, half], sent.at[8], recv.at[6], sibling)
    wait_bytes(sbuf.at[pl.ds(0, peers)], sent.at[3])
    wait_bytes(pbuf.at[0, pl.ds(0, peers)], sent.at[4])
    wait_bytes(pbuf.at[0, pl.ds(0, peers)], sent.at[9])
    get_wo.wait()
    total = jnp.dot(obuf[0], wo[0], preferred_element_type=F32)
    wait_bytes(wo.at[far, half], recv.at[6])
    for dt in (1, 3, 2):
        wait_bytes(obuf.at[0], orecv.at[dt])
        total += jnp.dot(obuf[dt], wo[dt], preferred_element_type=F32)
    rounded = total.astype(BF)
    for piece in range(2):
        for kind in range(2):
            at = piece * TOK + kind * HALF
            out[kind * TOK + piece * HALF : kind * TOK + (piece + 1) * HALF, :] = rounded[at : at + HALF, :]
    wait_bytes(wo.at[far, quarter], sent.at[5])
    wait_bytes(wo.at[far, pl.ds(0, 3 * TOK)], sent.at[7])
    wait_bytes(wo.at[far, half], sent.at[8])
    wait_bytes(obuf.at[far], sent.at[6])


def on_device(hidden_in, hidden_tan, qkv_weight, out_weight, norm_gain, pos_local, tile_anchor):
    quarter = HD // 4
    frequency = np.float32(THETA) ** (-np.arange(quarter, dtype=np.float32) / np.float32(quarter))
    freq = jnp.asarray(np.tile(frequency.astype(np.float32), (8, 4)))
    hbm = pl.BlockSpec(memory_space=pltpu.HBM)
    vmem = pl.BlockSpec(memory_space=pltpu.VMEM)
    dma = pltpu.SemaphoreType.DMA
    columns = NT * HD
    operands = (
        hidden_in, hidden_tan, qkv_weight, out_weight, norm_gain, pos_local,
        tile_anchor.reshape(1, 2), freq,
    )
    both = pl.pallas_call(
        kernel,
        out_shape=pltpu.VMEM((2 * TOK, columns), BF),
        in_specs=[hbm] * 8,
        out_specs=vmem,
        scratch_shapes=[
            pltpu.VMEM((2 * TOK, 2048), BF),
            pltpu.VMEM((3, 2048, 2 * HD), BF),
            pltpu.VMEM((NT, 2 * HD, columns), BF),
            pltpu.VMEM((2, HD), F32),
            pltpu.VMEM((2, TOK), jnp.int32),
            pltpu.VMEM((1, 2), jnp.int32),
            pltpu.VMEM((8, HD), F32),
            pltpu.VMEM((2, TOK, 2 * HD), BF),
            pltpu.VMEM((2, TOK, 2 * HD), BF),
            pltpu.VMEM((2, TOK, 2 * HD), BF),
            pltpu.VMEM((ROWS, 2 * HD), BF),
            pltpu.VMEM((ROWS, 2 * HD), BF),
            pltpu.VMEM((ROWS, 2 * HD), BF),
            pltpu.VMEM((ROWS, 2 * HD), BF),
            pltpu.VMEM((2 * NY, 1, HD), F32),
            pltpu.VMEM((2, 2 * NY, HALF, 2 * HD), BF),
            pltpu.VMEM((2 * NY, 1, HD), F32),
            pltpu.VMEM((NT, 2 * TOK, 2 * HD), BF),
            dma((10,)),
            dma((10,)),
            dma((9,)),
            dma((NT,)),
            pltpu.SemaphoreType.REGULAR((NT,)),
        ],
        compiler_params=pltpu.CompilerParams(
            collective_id=0, has_side_effects=True, vmem_limit_bytes=40 * 2**20
        ),
    )(*[pltpu.with_memory_space_constraint(a, pltpu.HBM) for a in operands])
    return both[:TOK], both[TOK:]


def solution(mesh):
    in_specs = (
        P("ctx", None),
        P("ctx", None),
        P(None, None, "tp"),
        P("tp", None),
        P(),
        P(None, "ctx"),
        P(None, "ctx"),
    )
    out_specs = (P("ctx", "tp"), P("ctx", "tp"))
    return jax.shard_map(
        on_device, mesh=mesh, in_specs=in_specs, out_specs=out_specs, check_vma=False
    )
```

```python
import functools

import numpy as np
import jax
import jax.numpy as jnp
from jax import lax
from jax.experimental import pallas as pl
from jax.experimental.pallas import tpu as pltpu
from jax.sharding import PartitionSpec as P

THETA = 10000.0
MESH = pl.DeviceIdType.MESH
BF = jnp.bfloat16
F32 = jnp.float32

TOK = 32
HALF = TOK // 2
HD = 128
NX, NY, NZ, NT = 4, 8, 2, 4
ROWS = NY * 2 * TOK
QB = 128
SCALE = HD**-0.5

XZ = [(2, 1), (1, 1), (3, 1), (2, 0), (1, 0), (3, 0), (0, 1), (0, 0)]
YS = [4, 3, 5, 2, 6, 1, 7, 0]


def slot_xz(dx, dz):
    return (dx % NX) * NZ + dz % NZ


def sin_cos(x):
    k = jnp.floor(x * 0.6366197723675814 + 0.5)
    r = ((x - k * 1.5703125) - k * 4.837512969970703125e-4) - k * 7.54978995489188216e-8
    r2 = r * r
    s = r + r * r2 * (-1.6666654611e-1 + r2 * (8.3321608736e-3 + r2 * -1.9515295891e-4))
    c = 1.0 - 0.5 * r2 + r2 * r2 * (
        4.166664568298827e-2 + r2 * (-1.388731625493765e-3 + r2 * 2.443315711809948e-5)
    )
    quad = k - 4.0 * jnp.floor(k * 0.25)
    odd = (quad == 1.0) | (quad == 3.0)
    sin = jnp.where(odd, c, s)
    cos = jnp.where(odd, s, c)
    sin = jnp.where(quad >= 2.0, -sin, sin)
    cos = jnp.where((quad == 1.0) | (quad == 2.0), -cos, cos)
    return sin, cos


def split(value):
    near = value.astype(BF)
    return near, (value - near.astype(F32)).astype(BF)


def kernel(
    hin, htan, wqkv, wout, gain, pos, anchor, freq,
    out,
    h, w, wo, gain_v, pos_v, anchor_v, freq_v,
    kmsg, qmsg, vmsg, kbuf, qbuf, vbuf, part, stat, pbuf, sbuf, obuf,
    loc, sent, recv, orecv, ready,
):
    ctx = lax.axis_index("ctx")
    tp = lax.axis_index("tp")
    z, x, y, core = ctx // 64, (ctx // 16) % NX, (ctx // 2) % NY, ctx % 2

    def chip_xz(dx, dz, c):
        return {"ctx": ((((z + dz) % NZ) * NX + (x + dx) % NX) * NY + y) * 2 + c}

    def chip_y(dy, c):
        return {"ctx": ((z * NX + x) * NY + (y + dy) % NY) * 2 + c}

    def peer_tp(dt):
        return {"tp": (tp + dt + NT) % NT}

    other = 1 - core
    sibling = {"ctx": ctx + 1 - 2 * core}

    barrier = pltpu.get_barrier_semaphore()
    count = 0
    for c in range(2):
        for dy in YS[:-1]:
            pl.semaphore_signal(barrier, inc=1, device_id=chip_y(dy, c), device_id_type=MESH)
            count += 1
        for dx, dz in XZ[:-1]:
            pl.semaphore_signal(barrier, inc=1, device_id=chip_xz(dx, dz, c), device_id_type=MESH)
            count += 1
    pl.semaphore_signal(barrier, inc=1, device_id=sibling, device_id_type=MESH)
    count += 1
    for k in (1, 2, 3):

        @pl.when(tp + k < NT)
        def _():
            pl.semaphore_signal(barrier, inc=1, device_id=peer_tp(k), device_id_type=MESH)


    def fetch(i, src, dst):
        copy = pltpu.make_async_copy(src, dst, loc.at[i])
        copy.start()
        return copy

    get_pos = fetch(0, pos, pos_v)
    get_anchor = fetch(1, anchor, anchor_v)
    get_freq = fetch(2, freq, freq_v)
    get_hin = fetch(3, hin, h.at[pl.ds(0, TOK)])
    get_htan = fetch(4, htan, h.at[pl.ds(TOK, TOK)])
    get_wk = fetch(5, wqkv.at[1], w.at[1])
    get_gain = fetch(6, gain, gain_v)
    get_wq = fetch(7, wqkv.at[0], w.at[0])
    get_wv = fetch(8, wqkv.at[2], w.at[2])
    columns = NT * HD
    get_wo = fetch(9, wout.at[:, pl.ds(pl.multiple_of(tp * columns, columns), columns)], wo.at[0])

    get_pos.wait()
    get_anchor.wait()
    get_freq.wait()
    row_place = pos_v[0:1, :] + anchor_v[:, 0:1]
    col_place = pos_v[1:2, :] + anchor_v[:, 1:2]
    eye = lax.broadcasted_iota(jnp.int32, (TOK, TOK), 0) == lax.broadcasted_iota(
        jnp.int32, (TOK, TOK), 1
    )
    row_id = jnp.sum(jnp.where(eye, row_place.astype(F32), 0.0), axis=1, keepdims=True)
    col_id = jnp.sum(jnp.where(eye, col_place.astype(F32), 0.0), axis=1, keepdims=True)
    lane = lax.broadcasted_iota(jnp.int32, (TOK, HD), 1)
    sine, cosine = sin_cos(jnp.where(lane < HD // 2, row_id, col_id) * freq_v[0:1, :])
    low = lane % (HD // 2) < HD // 4
    sine = jnp.where(low, -sine, sine)

    def rotate(n):
        wide = n.astype(BF).astype(F32)
        turned = jnp.where(low, pltpu.roll(wide, HD - HD // 4, 1), pltpu.roll(wide, HD // 4, 1))
        return (wide * cosine + turned * sine).astype(BF)

    def norm_rotate(projected, row, head):
        g = gain_v[row : row + 1, :]
        raw = projected[:TOK, head * HD : (head + 1) * HD]
        tan = projected[TOK:, head * HD : (head + 1) * HD]
        ms = jnp.mean(raw * raw, axis=1, keepdims=True) + 1e-06
        r = lax.rsqrt(ms)
        cross = jnp.mean(raw * tan, axis=1, keepdims=True)
        n = raw * r * g
        dn = g * r * (tan - raw * (cross / ms))
        return rotate(n), rotate(dn)

    def project(which):
        return jnp.dot(h[...], w[which], preferred_element_type=F32)

    def own_rows(slot):
        return pl.ds(pl.multiple_of(slot * 2 * TOK + core * TOK, TOK), TOK)

    def send(src, dst, ssem, rsem, device):
        copy = pltpu.make_async_remote_copy(
            src_ref=src, dst_ref=dst, send_sem=ssem, recv_sem=rsem,
            device_id=device, device_id_type=MESH,
        )
        copy.start()

    def spread_xz(msg, buf, ssem, rsem):
        for dx, dz in XZ:
            there = slot_xz(-dx, -dz)
            for flip in range(2):
                if (dx, dz) == (0, 0) and flip == 0:
                    continue
                c = core if flip == 0 else other
                send(
                    msg.at[c], buf.at[own_rows(there)],
                    ssem, rsem, chip_xz(dx, dz, c),
                )

    def spread_y(msg, buf, ssem, rsem):
        for dy in YS:
            there = (NY - dy) % NY
            for flip in range(2):
                if dy == 0 and flip == 0:
                    continue
                c = core if flip == 0 else other
                send(
                    msg.at[c], buf.at[own_rows(there)],
                    ssem, rsem, chip_y(dy, c),
                )

    def keep(msg, buf):
        buf[own_rows(0), :] = msg[core]

    def wait_bytes(ref, sem):
        pltpu.make_async_copy(ref, ref, sem).wait()

    peers = 2 * NY - 1

    def wait_all(buf, sem):
        wait_bytes(buf.at[pl.ds(0, peers * TOK)], sem)

    get_gain.wait()
    get_hin.wait()
    get_htan.wait()
    get_wk.wait()
    projected = project(1)
    for head in range(2):
        k, dk = norm_rotate(projected, 1, head)
        kmsg[head, :, :HD] = k
        kmsg[head, :, HD:] = dk
    pl.semaphore_wait(barrier, count + tp)
    for k in (3, 2, 1):

        @pl.when(tp >= k)
        def _():
            pl.semaphore_signal(ready.at[k], inc=1, device_id=peer_tp(-k), device_id_type=MESH)

    spread_xz(kmsg, kbuf, sent.at[0], recv.at[0])
    get_wq.wait()
    projected = project(0)
    for head in range(2):
        q, dq = norm_rotate(projected, 0, head)
        qmsg[head, :, :HD] = dq
        qmsg[head, :, HD:] = q
    spread_y(qmsg, qbuf, sent.at[1], recv.at[1])
    get_wv.wait()
    projected = project(2)
    for head in range(2):
        vmsg[head, :, :HD] = projected[:TOK, head * HD : (head + 1) * HD].astype(BF)
        vmsg[head, :, HD:] = projected[TOK:, head * HD : (head + 1) * HD].astype(BF)
    spread_xz(vmsg, vbuf, sent.at[2], recv.at[2])
    half = pl.ds(pl.multiple_of(core * HD, HD), HD)
    quarter = pl.ds(pl.multiple_of(core * HD + x * TOK, TOK), TOK)
    far = pl.ds(1, NT - 1)

    def send_columns(dt):
        to = (tp + dt + NT) % NT
        send(
            wout.at[quarter, pl.ds(pl.multiple_of(to * columns, columns), columns)],
            wo.at[(NT - dt) % NT, quarter], sent.at[5], recv.at[5], peer_tp(dt),
        )

    for k in (3, 2, 1):
        pl.when(tp >= k)(functools.partial(send_columns, -k))

    keep(kmsg, kbuf)
    keep(qmsg, qbuf)
    keep(vmsg, vbuf)

    wait_all(kbuf, recv.at[0])
    wait_all(qbuf, recv.at[1])
    wait_all(vbuf, recv.at[2])

    nt = (((1,), (1,)), ((), ()))
    blocks = ROWS // QB
    lane_s = lax.broadcasted_iota(jnp.int32, (QB, HD), 1)
    for b in (2, 1, 3, 0):
        rows = pl.ds(b * QB, QB)
        s = lax.dot_general(qbuf[rows, HD:], kbuf[:, :HD], nt, preferred_element_type=F32) * SCALE
        ds = lax.dot_general(qbuf[rows, :], kbuf[...], nt, preferred_element_type=F32) * SCALE
        m = jnp.max(s, axis=1, keepdims=True)
        e = jnp.exp(s - m)
        weighted = e * ds
        l = jnp.sum(e, axis=1, keepdims=True)
        g = jnp.sum(weighted, axis=1, keepdims=True)
        e, e_rest = split(e)
        weighted, weighted_rest = split(weighted)
        both = jnp.dot(e, vbuf[...], preferred_element_type=F32)
        both += jnp.dot(e_rest, vbuf[...], preferred_element_type=F32)
        mix = jnp.dot(weighted, vbuf[:, :HD], preferred_element_type=F32)
        mix += jnp.dot(weighted_rest, vbuf[:, :HD], preferred_element_type=F32)
        inv = 1.0 / l
        slope = g * inv
        o = both[:, :HD] * inv
        part[rows, :HD] = o.astype(BF)
        part[rows, HD:] = ((both[:, HD:] + mix) * inv - slope * o).astype(BF)
        packed = jnp.where(lane_s == 0, m, jnp.where(lane_s == 1, l, jnp.where(lane_s == 2, slope, 0.0)))
        lines = packed.T[:8, :]
        turns = [lines] + [pltpu.roll(lines, HD - TOK * k, 1) for k in range(1, 4)]
        for j in range(4):
            stat[4 * b + j] = jnp.where(
                lane_s[:1] < TOK,
                turns[j][0:1],
                jnp.where(lane_s[:1] < 2 * TOK, turns[(j + 3) % 4][1:2], turns[(j + 2) % 4][2:3]),
            )
        for dy in (2 * b, 2 * b + 1):
            there = (NY - dy) % NY
            for flip in range(2):
                if dy == 0 and flip == 0:
                    continue
                c = core if flip == 0 else other
                src = pl.ds(pl.multiple_of(dy * 2 * TOK + c * TOK, HALF), HALF)
                send(
                    stat.at[2 * dy + c], sbuf.at[core * NY + there],
                    sent.at[3], recv.at[3], chip_y(dy, c),
                )
                send(
                    part.at[src], pbuf.at[0, core * NY + there],
                    sent.at[4], recv.at[4], chip_y(dy, c),
                )
    for dy in (4, 5, 2, 3, 6, 7, 1, 0):
        there = (NY - dy) % NY
        for flip in range(2):
            if dy == 0 and flip == 0:
                continue
            c = core if flip == 0 else other
            src = pl.ds(pl.multiple_of(dy * 2 * TOK + c * TOK + HALF, HALF), HALF)
            send(
                part.at[src], pbuf.at[1, core * NY + there],
                sent.at[9], recv.at[8], chip_y(dy, c),
            )
    for piece in range(2):
        own = pl.ds(pl.multiple_of(core * TOK + piece * HALF, HALF), HALF)
        pbuf[piece, core * NY] = part[own, :]
    sbuf[core * NY] = stat[core]

    for k in (1, 2, 3):

        @pl.when(tp + k < NT)
        def _():
            pl.semaphore_wait(ready.at[k], 1)
            send_columns(k)

    wait_bytes(wo.at[far, quarter], recv.at[5])
    for dx in (2, 1, 3):
        send(wo.at[far, quarter], wo.at[far, quarter], sent.at[7], recv.at[7], chip_xz(dx, 0, core))

    wait_all(kbuf, sent.at[0])
    wait_all(qbuf, sent.at[1])
    wait_all(vbuf, sent.at[2])

    wait_bytes(sbuf.at[pl.ds(0, peers)], recv.at[3])
    coefs = []
    for head in range(2):
        m = jnp.concatenate([sbuf[head * NY + slot] for slot in range(NY)], 0)
        l = pltpu.roll(m, HD - TOK, 1)
        slope = pltpu.roll(m, HD - 2 * TOK, 1)
        top = jnp.max(m, axis=0, keepdims=True)
        weight = jnp.exp(m - top) * l
        weight = weight / jnp.sum(weight, axis=0, keepdims=True)
        mean_slope = jnp.sum(weight * slope, axis=0, keepdims=True)
        coefs += [weight, weight * (slope - mean_slope)]
    coefs.append(jnp.zeros((HD - 4 * NY, HD), F32))
    table = jnp.concatenate(coefs, 0).T[:TOK, :]
    for piece in range(2):
        wait_bytes(pbuf.at[0, pl.ds(0, peers)], recv.at[4 if piece == 0 else 8])
        for head in range(2):
            o = jnp.zeros((HALF, HD), F32)
            do = jnp.zeros((HALF, HD), F32)
            for slot in range(NY):
                at = head * 2 * NY + slot
                a = table[piece * HALF : (piece + 1) * HALF, at : at + 1]
                b = table[piece * HALF : (piece + 1) * HALF, at + NY : at + NY + 1]
                value = pbuf[piece, head * NY + slot, :, :HD].astype(F32)
                o += a * value
                do += a * pbuf[piece, head * NY + slot, :, HD:].astype(F32) + b * value
            obuf[0, piece * TOK : piece * TOK + HALF, head * HD : (head + 1) * HD] = o.astype(BF)
            obuf[0, piece * TOK + HALF : (piece + 1) * TOK, head * HD : (head + 1) * HD] = do.astype(BF)
        rows = pl.ds(piece * TOK, TOK)

        def send_rows(dt, rows):
            send(
                obuf.at[0, rows], obuf.at[(NT - dt) % NT, rows],
                sent.at[6], orecv.at[(NT - dt) % NT], peer_tp(dt),
            )

        for k in (3, 2, 1):
            pl.when(tp >= k)(functools.partial(send_rows, -k, rows))
    for k in (1, 2, 3):

        @pl.when(tp + k < NT)
        def _():
            send_rows(k, pl.ds(0, 2 * TOK))


    wait_bytes(wo.at[far, pl.ds(0, 3 * TOK)], recv.at[7])
    send(wo.at[far, half], wo.at[far, half], sent.at[8], recv.at[6], sibling)
    wait_bytes(sbuf.at[pl.ds(0, peers)], sent.at[3])
    wait_bytes(pbuf.at[0, pl.ds(0, peers)], sent.at[4])
    wait_bytes(pbuf.at[0, pl.ds(0, peers)], sent.at[9])
    get_wo.wait()
    total = jnp.dot(obuf[0], wo[0], preferred_element_type=F32)
    wait_bytes(wo.at[far, half], recv.at[6])
    for dt in (1, 3, 2):
        wait_bytes(obuf.at[0], orecv.at[dt])
        total += jnp.dot(obuf[dt], wo[dt], preferred_element_type=F32)
    rounded = total.astype(BF)
    for piece in range(2):
        for kind in range(2):
            at = piece * TOK + kind * HALF
            out[kind * TOK + piece * HALF : kind * TOK + (piece + 1) * HALF, :] = rounded[at : at + HALF, :]
    wait_bytes(wo.at[far, quarter], sent.at[5])
    wait_bytes(wo.at[far, pl.ds(0, 3 * TOK)], sent.at[7])
    wait_bytes(wo.at[far, half], sent.at[8])
    wait_bytes(obuf.at[far], sent.at[6])


def on_device(hidden_in, hidden_tan, qkv_weight, out_weight, norm_gain, pos_local, tile_anchor):
    quarter = HD // 4
    frequency = np.float32(THETA) ** (-np.arange(quarter, dtype=np.float32) / np.float32(quarter))
    freq = jnp.asarray(np.tile(frequency.astype(np.float32), (8, 4)))
    hbm = pl.BlockSpec(memory_space=pltpu.HBM)
    vmem = pl.BlockSpec(memory_space=pltpu.VMEM)
    dma = pltpu.SemaphoreType.DMA
    columns = NT * HD
    operands = (
        hidden_in, hidden_tan, qkv_weight, out_weight, norm_gain, pos_local,
        tile_anchor.reshape(1, 2), freq,
    )
    both = pl.pallas_call(
        kernel,
        out_shape=pltpu.VMEM((2 * TOK, columns), BF),
        in_specs=[hbm] * 8,
        out_specs=vmem,
        scratch_shapes=[
            pltpu.VMEM((2 * TOK, 2048), BF),
            pltpu.VMEM((3, 2048, 2 * HD), BF),
            pltpu.VMEM((NT, 2 * HD, columns), BF),
            pltpu.VMEM((2, HD), F32),
            pltpu.VMEM((2, TOK), jnp.int32),
            pltpu.VMEM((1, 2), jnp.int32),
            pltpu.VMEM((8, HD), F32),
            pltpu.VMEM((2, TOK, 2 * HD), BF),
            pltpu.VMEM((2, TOK, 2 * HD), BF),
            pltpu.VMEM((2, TOK, 2 * HD), BF),
            pltpu.VMEM((ROWS, 2 * HD), BF),
            pltpu.VMEM((ROWS, 2 * HD), BF),
            pltpu.VMEM((ROWS, 2 * HD), BF),
            pltpu.VMEM((ROWS, 2 * HD), BF),
            pltpu.VMEM((2 * NY, 1, HD), F32),
            pltpu.VMEM((2, 2 * NY, HALF, 2 * HD), BF),
            pltpu.VMEM((2 * NY, 1, HD), F32),
            pltpu.VMEM((NT, 2 * TOK, 2 * HD), BF),
            dma((10,)),
            dma((10,)),
            dma((9,)),
            dma((NT,)),
            pltpu.SemaphoreType.REGULAR((NT,)),
        ],
        compiler_params=pltpu.CompilerParams(
            collective_id=0, has_side_effects=True, vmem_limit_bytes=40 * 2**20
        ),
    )(*[pltpu.with_memory_space_constraint(a, pltpu.HBM) for a in operands])
    return both[:TOK], both[TOK:]


def solution(mesh):
    in_specs = (
        P("ctx", None),
        P("ctx", None),
        P(None, None, "tp"),
        P("tp", None),
        P(),
        P(None, "ctx"),
        P(None, "ctx"),
    )
    out_specs = (P("ctx", "tp"), P("ctx", "tp"))
    return jax.shard_map(
        on_device, mesh=mesh, in_specs=in_specs, out_specs=out_specs, check_vma=False
    )
```

```python
import functools

import numpy as np
import jax
import jax.numpy as jnp
from jax import lax
from jax.experimental import pallas as pl
from jax.experimental.pallas import tpu as pltpu
from jax.sharding import PartitionSpec as P

THETA = 10000.0
MESH = pl.DeviceIdType.MESH
BF = jnp.bfloat16
F32 = jnp.float32

TOK = 32
HALF = TOK // 2
HD = 128
NX, NY, NZ, NT = 4, 8, 2, 4
ROWS = NY * 2 * TOK
QB = 128
SCALE = HD**-0.5

XZ = [(2, 1), (1, 1), (3, 1), (2, 0), (1, 0), (3, 0), (0, 1), (0, 0)]
YS = [4, 3, 5, 2, 6, 1, 7, 0]


def slot_xz(dx, dz):
    return (dx % NX) * NZ + dz % NZ


def sin_cos(x):
    k = jnp.floor(x * 0.6366197723675814 + 0.5)
    r = ((x - k * 1.5703125) - k * 4.837512969970703125e-4) - k * 7.54978995489188216e-8
    r2 = r * r
    s = r + r * r2 * (-1.6666654611e-1 + r2 * (8.3321608736e-3 + r2 * -1.9515295891e-4))
    c = 1.0 - 0.5 * r2 + r2 * r2 * (
        4.166664568298827e-2 + r2 * (-1.388731625493765e-3 + r2 * 2.443315711809948e-5)
    )
    quad = k - 4.0 * jnp.floor(k * 0.25)
    odd = (quad == 1.0) | (quad == 3.0)
    sin = jnp.where(odd, c, s)
    cos = jnp.where(odd, s, c)
    sin = jnp.where(quad >= 2.0, -sin, sin)
    cos = jnp.where((quad == 1.0) | (quad == 2.0), -cos, cos)
    return sin, cos


def split(value):
    near = value.astype(BF)
    return near, (value - near.astype(F32)).astype(BF)


def kernel(
    hin, htan, wqkv, wout, gain, pos, anchor, freq,
    out,
    h, w, wo, gain_v, pos_v, anchor_v, freq_v,
    kmsg, qmsg, vmsg, kbuf, qbuf, vbuf, part, stat, pbuf, sbuf, obuf,
    loc, sent, recv, orecv, ready,
):
    ctx = lax.axis_index("ctx")
    tp = lax.axis_index("tp")
    z, x, y, core = ctx // 64, (ctx // 16) % NX, (ctx // 2) % NY, ctx % 2

    def chip_xz(dx, dz, c):
        return {"ctx": ((((z + dz) % NZ) * NX + (x + dx) % NX) * NY + y) * 2 + c}

    def chip_y(dy, c):
        return {"ctx": ((z * NX + x) * NY + (y + dy) % NY) * 2 + c}

    def peer_tp(dt):
        return {"tp": (tp + dt + NT) % NT}

    other = 1 - core
    sibling = {"ctx": ctx + 1 - 2 * core}

    def fetch(i, src, dst):
        copy = pltpu.make_async_copy(src, dst, loc.at[i])
        copy.start()
        return copy

    get_pos = fetch(0, pos, pos_v)
    get_anchor = fetch(1, anchor, anchor_v)
    get_freq = fetch(2, freq, freq_v)
    get_hin = fetch(3, hin, h.at[pl.ds(0, TOK)])
    get_htan = fetch(4, htan, h.at[pl.ds(TOK, TOK)])
    get_wk = fetch(5, wqkv.at[1], w.at[1])
    get_gain = fetch(6, gain, gain_v)
    get_wq = fetch(7, wqkv.at[0], w.at[0])
    get_wv = fetch(8, wqkv.at[2], w.at[2])
    columns = NT * HD
    get_wo = fetch(9, wout.at[:, pl.ds(pl.multiple_of(tp * columns, columns), columns)], wo.at[0])

    barrier = pltpu.get_barrier_semaphore()
    count = 0
    for c in range(2):
        for dy in YS[:-1]:
            pl.semaphore_signal(barrier, inc=1, device_id=chip_y(dy, c), device_id_type=MESH)
            count += 1
        for dx, dz in XZ[:-1]:
            pl.semaphore_signal(barrier, inc=1, device_id=chip_xz(dx, dz, c), device_id_type=MESH)
            count += 1
    pl.semaphore_signal(barrier, inc=1, device_id=sibling, device_id_type=MESH)
    count += 1
    for k in (1, 2, 3):

        @pl.when(tp + k < NT)
        def _():
            pl.semaphore_signal(barrier, inc=1, device_id=peer_tp(k), device_id_type=MESH)


    get_pos.wait()
    get_anchor.wait()
    get_freq.wait()
    row_place = pos_v[0:1, :] + anchor_v[:, 0:1]
    col_place = pos_v[1:2, :] + anchor_v[:, 1:2]
    eye = lax.broadcasted_iota(jnp.int32, (TOK, TOK), 0) == lax.broadcasted_iota(
        jnp.int32, (TOK, TOK), 1
    )
    row_id = jnp.sum(jnp.where(eye, row_place.astype(F32), 0.0), axis=1, keepdims=True)
    col_id = jnp.sum(jnp.where(eye, col_place.astype(F32), 0.0), axis=1, keepdims=True)
    lane = lax.broadcasted_iota(jnp.int32, (TOK, HD), 1)
    sine, cosine = sin_cos(jnp.where(lane < HD // 2, row_id, col_id) * freq_v[0:1, :])
    low = lane % (HD // 2) < HD // 4
    sine = jnp.where(low, -sine, sine)

    def rotate(n):
        wide = n.astype(BF).astype(F32)
        turned = jnp.where(low, pltpu.roll(wide, HD - HD // 4, 1), pltpu.roll(wide, HD // 4, 1))
        return (wide * cosine + turned * sine).astype(BF)

    def norm_rotate(projected, row, head):
        g = gain_v[row : row + 1, :]
        raw = projected[:TOK, head * HD : (head + 1) * HD]
        tan = projected[TOK:, head * HD : (head + 1) * HD]
        ms = jnp.mean(raw * raw, axis=1, keepdims=True) + 1e-06
        r = lax.rsqrt(ms)
        cross = jnp.mean(raw * tan, axis=1, keepdims=True)
        n = raw * r * g
        dn = g * r * (tan - raw * (cross / ms))
        return rotate(n), rotate(dn)

    def project(which):
        return jnp.dot(h[...], w[which], preferred_element_type=F32)

    def own_rows(slot):
        return pl.ds(pl.multiple_of(slot * 2 * TOK + core * TOK, TOK), TOK)

    def send(src, dst, ssem, rsem, device):
        copy = pltpu.make_async_remote_copy(
            src_ref=src, dst_ref=dst, send_sem=ssem, recv_sem=rsem,
            device_id=device, device_id_type=MESH,
        )
        copy.start()

    def spread_xz(msg, buf, ssem, rsem):
        for dx, dz in XZ:
            there = slot_xz(-dx, -dz)
            for flip in range(2):
                if (dx, dz) == (0, 0) and flip == 0:
                    continue
                c = core if flip == 0 else other
                send(
                    msg.at[c], buf.at[own_rows(there)],
                    ssem, rsem, chip_xz(dx, dz, c),
                )

    def spread_y(msg, buf, ssem, rsem):
        for dy in YS:
            there = (NY - dy) % NY
            for flip in range(2):
                if dy == 0 and flip == 0:
                    continue
                c = core if flip == 0 else other
                send(
                    msg.at[c], buf.at[own_rows(there)],
                    ssem, rsem, chip_y(dy, c),
                )

    def keep(msg, buf):
        buf[own_rows(0), :] = msg[core]

    def wait_bytes(ref, sem):
        pltpu.make_async_copy(ref, ref, sem).wait()

    peers = 2 * NY - 1

    def wait_all(buf, sem):
        wait_bytes(buf.at[pl.ds(0, peers * TOK)], sem)

    get_gain.wait()
    get_hin.wait()
    get_htan.wait()
    get_wk.wait()
    projected = project(1)
    for head in range(2):
        k, dk = norm_rotate(projected, 1, head)
        kmsg[head, :, :HD] = k
        kmsg[head, :, HD:] = dk
    pl.semaphore_wait(barrier, count + tp)
    for k in (3, 2, 1):

        @pl.when(tp >= k)
        def _():
            pl.semaphore_signal(ready.at[k], inc=1, device_id=peer_tp(-k), device_id_type=MESH)

    spread_xz(kmsg, kbuf, sent.at[0], recv.at[0])
    get_wq.wait()
    projected = project(0)
    for head in range(2):
        q, dq = norm_rotate(projected, 0, head)
        qmsg[head, :, :HD] = dq
        qmsg[head, :, HD:] = q
    spread_y(qmsg, qbuf, sent.at[1], recv.at[1])
    get_wv.wait()
    projected = project(2)
    for head in range(2):
        vmsg[head, :, :HD] = projected[:TOK, head * HD : (head + 1) * HD].astype(BF)
        vmsg[head, :, HD:] = projected[TOK:, head * HD : (head + 1) * HD].astype(BF)
    spread_xz(vmsg, vbuf, sent.at[2], recv.at[2])
    half = pl.ds(pl.multiple_of(core * HD, HD), HD)
    quarter = pl.ds(pl.multiple_of(core * HD + x * TOK, TOK), TOK)
    far = pl.ds(1, NT - 1)

    def send_columns(dt):
        to = (tp + dt + NT) % NT
        send(
            wout.at[quarter, pl.ds(pl.multiple_of(to * columns, columns), columns)],
            wo.at[(NT - dt) % NT, quarter], sent.at[5], recv.at[5], peer_tp(dt),
        )

    for k in (3, 2, 1):
        pl.when(tp >= k)(functools.partial(send_columns, -k))

    keep(kmsg, kbuf)
    keep(qmsg, qbuf)
    keep(vmsg, vbuf)

    wait_all(kbuf, recv.at[0])
    wait_all(qbuf, recv.at[1])
    wait_all(vbuf, recv.at[2])

    nt = (((1,), (1,)), ((), ()))
    blocks = ROWS // QB
    lane_s = lax.broadcasted_iota(jnp.int32, (QB, HD), 1)
    for b in (2, 1, 3, 0):
        rows = pl.ds(b * QB, QB)
        s = lax.dot_general(qbuf[rows, HD:], kbuf[:, :HD], nt, preferred_element_type=F32) * SCALE
        ds = lax.dot_general(qbuf[rows, :], kbuf[...], nt, preferred_element_type=F32) * SCALE
        m = jnp.max(s, axis=1, keepdims=True)
        e = jnp.exp(s - m)
        weighted = e * ds
        l = jnp.sum(e, axis=1, keepdims=True)
        g = jnp.sum(weighted, axis=1, keepdims=True)
        e, e_rest = split(e)
        weighted, weighted_rest = split(weighted)
        both = jnp.dot(e, vbuf[...], preferred_element_type=F32)
        both += jnp.dot(e_rest, vbuf[...], preferred_element_type=F32)
        mix = jnp.dot(weighted, vbuf[:, :HD], preferred_element_type=F32)
        mix += jnp.dot(weighted_rest, vbuf[:, :HD], preferred_element_type=F32)
        inv = 1.0 / l
        slope = g * inv
        o = both[:, :HD] * inv
        part[rows, :HD] = o.astype(BF)
        part[rows, HD:] = ((both[:, HD:] + mix) * inv - slope * o).astype(BF)
        packed = jnp.where(lane_s == 0, m, jnp.where(lane_s == 1, l, jnp.where(lane_s == 2, slope, 0.0)))
        lines = packed.T[:8, :]
        turns = [lines] + [pltpu.roll(lines, HD - TOK * k, 1) for k in range(1, 4)]
        for j in range(4):
            stat[4 * b + j] = jnp.where(
                lane_s[:1] < TOK,
                turns[j][0:1],
                jnp.where(lane_s[:1] < 2 * TOK, turns[(j + 3) % 4][1:2], turns[(j + 2) % 4][2:3]),
            )
        for dy in (2 * b, 2 * b + 1):
            there = (NY - dy) % NY
            for flip in range(2):
                if dy == 0 and flip == 0:
                    continue
                c = core if flip == 0 else other
                src = pl.ds(pl.multiple_of(dy * 2 * TOK + c * TOK, HALF), HALF)
                send(
                    stat.at[2 * dy + c], sbuf.at[core * NY + there],
                    sent.at[3], recv.at[3], chip_y(dy, c),
                )
                send(
                    part.at[src], pbuf.at[0, core * NY + there],
                    sent.at[4], recv.at[4], chip_y(dy, c),
                )
    for dy in (4, 5, 2, 3, 6, 7, 1, 0):
        there = (NY - dy) % NY
        for flip in range(2):
            if dy == 0 and flip == 0:
                continue
            c = core if flip == 0 else other
            src = pl.ds(pl.multiple_of(dy * 2 * TOK + c * TOK + HALF, HALF), HALF)
            send(
                part.at[src], pbuf.at[1, core * NY + there],
                sent.at[9], recv.at[8], chip_y(dy, c),
            )
    for piece in range(2):
        own = pl.ds(pl.multiple_of(core * TOK + piece * HALF, HALF), HALF)
        pbuf[piece, core * NY] = part[own, :]
    sbuf[core * NY] = stat[core]

    for k in (1, 2, 3):

        @pl.when(tp + k < NT)
        def _():
            pl.semaphore_wait(ready.at[k], 1)
            send_columns(k)

    wait_bytes(wo.at[far, quarter], recv.at[5])
    for dx in (2, 1, 3):
        send(wo.at[far, quarter], wo.at[far, quarter], sent.at[7], recv.at[7], chip_xz(dx, 0, core))

    wait_all(kbuf, sent.at[0])
    wait_all(qbuf, sent.at[1])
    wait_all(vbuf, sent.at[2])

    wait_bytes(sbuf.at[pl.ds(0, peers)], recv.at[3])
    coefs = []
    for head in range(2):
        m = jnp.concatenate([sbuf[head * NY + slot] for slot in range(NY)], 0)
        l = pltpu.roll(m, HD - TOK, 1)
        slope = pltpu.roll(m, HD - 2 * TOK, 1)
        top = jnp.max(m, axis=0, keepdims=True)
        weight = jnp.exp(m - top) * l
        weight = weight / jnp.sum(weight, axis=0, keepdims=True)
        mean_slope = jnp.sum(weight * slope, axis=0, keepdims=True)
        coefs += [weight, weight * (slope - mean_slope)]
    coefs.append(jnp.zeros((HD - 4 * NY, HD), F32))
    table = jnp.concatenate(coefs, 0).T[:TOK, :]
    for piece in range(2):
        wait_bytes(pbuf.at[0, pl.ds(0, peers)], recv.at[4 if piece == 0 else 8])
        for head in range(2):
            o = jnp.zeros((HALF, HD), F32)
            do = jnp.zeros((HALF, HD), F32)
            for slot in range(NY):
                at = head * 2 * NY + slot
                a = table[piece * HALF : (piece + 1) * HALF, at : at + 1]
                b = table[piece * HALF : (piece + 1) * HALF, at + NY : at + NY + 1]
                value = pbuf[piece, head * NY + slot, :, :HD].astype(F32)
                o += a * value
                do += a * pbuf[piece, head * NY + slot, :, HD:].astype(F32) + b * value
            obuf[0, piece * TOK : piece * TOK + HALF, head * HD : (head + 1) * HD] = o.astype(BF)
            obuf[0, piece * TOK + HALF : (piece + 1) * TOK, head * HD : (head + 1) * HD] = do.astype(BF)
        rows = pl.ds(piece * TOK, TOK)

        def send_rows(dt, rows):
            send(
                obuf.at[0, rows], obuf.at[(NT - dt) % NT, rows],
                sent.at[6], orecv.at[(NT - dt) % NT], peer_tp(dt),
            )

        for k in (3, 2, 1):
            pl.when(tp >= k)(functools.partial(send_rows, -k, rows))
    for k in (1, 2, 3):

        @pl.when(tp + k < NT)
        def _():
            send_rows(k, pl.ds(0, 2 * TOK))


    wait_bytes(wo.at[far, pl.ds(0, 3 * TOK)], recv.at[7])
    send(wo.at[far, half], wo.at[far, half], sent.at[8], recv.at[6], sibling)
    wait_bytes(sbuf.at[pl.ds(0, peers)], sent.at[3])
    wait_bytes(pbuf.at[0, pl.ds(0, peers)], sent.at[4])
    wait_bytes(pbuf.at[0, pl.ds(0, peers)], sent.at[9])
    get_wo.wait()
    total = jnp.dot(obuf[0], wo[0], preferred_element_type=F32)
    wait_bytes(wo.at[far, half], recv.at[6])
    for dt in (1, 3, 2):
        wait_bytes(obuf.at[0], orecv.at[dt])
        total += jnp.dot(obuf[dt], wo[dt], preferred_element_type=F32)
    rounded = total.astype(BF)
    for piece in range(2):
        for kind in range(2):
            at = piece * TOK + kind * HALF
            out[kind * TOK + piece * HALF : kind * TOK + (piece + 1) * HALF, :] = rounded[at : at + HALF, :]
    wait_bytes(wo.at[far, quarter], sent.at[5])
    wait_bytes(wo.at[far, pl.ds(0, 3 * TOK)], sent.at[7])
    wait_bytes(wo.at[far, half], sent.at[8])
    wait_bytes(obuf.at[far], sent.at[6])


def on_device(hidden_in, hidden_tan, qkv_weight, out_weight, norm_gain, pos_local, tile_anchor):
    quarter = HD // 4
    frequency = np.float32(THETA) ** (-np.arange(quarter, dtype=np.float32) / np.float32(quarter))
    freq = jnp.asarray(np.tile(frequency.astype(np.float32), (8, 4)))
    hbm = pl.BlockSpec(memory_space=pltpu.HBM)
    vmem = pl.BlockSpec(memory_space=pltpu.VMEM)
    dma = pltpu.SemaphoreType.DMA
    columns = NT * HD
    operands = (
        hidden_in, hidden_tan, qkv_weight, out_weight, norm_gain, pos_local,
        tile_anchor.reshape(1, 2), freq,
    )
    both = pl.pallas_call(
        kernel,
        out_shape=pltpu.VMEM((2 * TOK, columns), BF),
        in_specs=[hbm] * 8,
        out_specs=vmem,
        scratch_shapes=[
            pltpu.VMEM((2 * TOK, 2048), BF),
            pltpu.VMEM((3, 2048, 2 * HD), BF),
            pltpu.VMEM((NT, 2 * HD, columns), BF),
            pltpu.VMEM((2, HD), F32),
            pltpu.VMEM((2, TOK), jnp.int32),
            pltpu.VMEM((1, 2), jnp.int32),
            pltpu.VMEM((8, HD), F32),
            pltpu.VMEM((2, TOK, 2 * HD), BF),
            pltpu.VMEM((2, TOK, 2 * HD), BF),
            pltpu.VMEM((2, TOK, 2 * HD), BF),
            pltpu.VMEM((ROWS, 2 * HD), BF),
            pltpu.VMEM((ROWS, 2 * HD), BF),
            pltpu.VMEM((ROWS, 2 * HD), BF),
            pltpu.VMEM((ROWS, 2 * HD), BF),
            pltpu.VMEM((2 * NY, 1, HD), F32),
            pltpu.VMEM((2, 2 * NY, HALF, 2 * HD), BF),
            pltpu.VMEM((2 * NY, 1, HD), F32),
            pltpu.VMEM((NT, 2 * TOK, 2 * HD), BF),
            dma((10,)),
            dma((10,)),
            dma((9,)),
            dma((NT,)),
            pltpu.SemaphoreType.REGULAR((NT,)),
        ],
        compiler_params=pltpu.CompilerParams(
            collective_id=0, has_side_effects=True, vmem_limit_bytes=40 * 2**20
        ),
    )(*[pltpu.with_memory_space_constraint(a, pltpu.HBM) for a in operands])
    return both[:TOK], both[TOK:]


def solution(mesh):
    in_specs = (
        P("ctx", None),
        P("ctx", None),
        P(None, None, "tp"),
        P("tp", None),
        P(),
        P(None, "ctx"),
        P(None, "ctx"),
    )
    out_specs = (P("ctx", "tp"), P("ctx", "tp"))
    return jax.shard_map(
        on_device, mesh=mesh, in_specs=in_specs, out_specs=out_specs, check_vma=False
    )
```
